128 devices in a mesh: node: 16 (over y, x), local: 8 (over z, core).
Axes of the slice: x: 4, y: 4, z: 4, core: 2. Of those that a mesh axis runs over, the one named last changes fastest.
Arguments:
- tokens_x: bfloat16 [16384, 2048], P(('node', 'local')), may hold values from -6 to 6
- grad_out: bfloat16 [16384, 2048], P(('node', 'local')), may hold values from -6 to 6
- expert_ids: int32 [16384, 8], P(('node', 'local')), may hold values from 0 to 127, all different within a row; in each aligned block of 128 rows (0 to 127, 128 to 255, ...) at most 9 rows name the same one
- probs: bfloat16 [16384, 8], P(('node', 'local')), may hold values from 0.049804688 to 0.34960938
- w_gate: bfloat16 [128, 2048, 768], P(('node', 'local')), may hold values from -0.125 to 0.125
- w_up: bfloat16 [128, 2048, 768], P(('node', 'local')), may hold values from -0.125 to 0.125
- w_down: bfloat16 [128, 768, 2048], P(('node', 'local')), may hold values from -0.21875 to 0.21875
Outputs:
- grad_x: bfloat16 [16384, 2048], P(('node', 'local'))
- grad_probs: bfloat16 [16384, 8], P(('node', 'local'))
- grad_gate: bfloat16 [128, 2048, 768], P(('node', 'local'))
- grad_up: bfloat16 [128, 2048, 768], P(('node', 'local'))
- grad_down: bfloat16 [128, 768, 2048], P(('node', 'local'))
The draws below stay inside these ranges and needn't reach their ends.
Inputs may be any that keep to these rules, and one draw needn't show every extreme that they name: `expert_ids`: each row names 8 different experts; among the 128 tokens of one device no expert is named more than 9 times, a bound that some block reaches.
All inputs are finite; a program needn't handle non-finite values.
Results may differ from the reference program's by a relative error of at most 0.0065.
Values may be sent and summed in bfloat16 or wider, within the bound.
A program may use at most 128 MiB of HBM per device.

```python
import math
import jax
import jax.numpy as jnp
import numpy as np
from jax import lax

D = 2048
FF = 768
TOP = 8
TOK_DEV = 128
EXPERTS = 128
TOKENS = 16384
CAP = 9
N_NODE = 16
N_LOCAL = 8


def shard_levels(key, extent, cuts, least, top_value):
    gain, own = 1.0, jax.random.fold_in(key, 6)
    for position, shards_of in cuts:
        steps = jnp.exp(jax.random.uniform(jax.random.fold_in(own, position), (shards_of,), jnp.float32, least / len(cuts), top_value / len(cuts)))
        gain = gain * jnp.repeat(steps, extent[position] // shards_of).reshape([-1 if axis == position else 1 for axis in range(len(extent))])
    return gain


def routed_block(rng, own, number, rows, number_of, top, reach, skew):
    order = jax.random.permutation(rng, number_of)
    packed, ordinary = portions_of(number_of, rows * top, reach, skew, True), portions_of(number_of, rows * top, reach, skew, False)
    places = jnp.arange(number_of)

    def named(lengths, turn):
        used = int((lengths > 0).sum())
        fixed = max(1, used // 4)
        passed = fixed + (places - fixed + turn * (used - fixed)) % max(1, number_of - fixed)
        return jnp.zeros((number_of,), jnp.int32).at[order[jnp.where(places < fixed, places, passed)]].set(jnp.asarray(lengths, jnp.int32))

    lengths = jnp.where(number % 4 == 0, named(packed, number // 4), named(ordinary, number - number // 4 - 1))
    mixed = jax.random.permutation(jax.random.fold_in(own, 3), number_of)
    giver, receiver = mixed[0:number_of // 2 * 2:2], mixed[1:number_of // 2 * 2:2]
    room = jnp.minimum(lengths[giver] - 1, reach - lengths[receiver]) // 2
    room = jnp.where((giver == order[0]) | (receiver == order[0]) | (lengths[receiver] == 0), 0, jnp.maximum(room, 0))
    passed = jax.random.randint(jax.random.fold_in(own, 4), (number_of // 2,), 0, 1 << 20) % (room + 1)
    lengths = lengths.at[giver].add(-passed).at[receiver].add(passed)
    members = jnp.searchsorted(jnp.cumsum(lengths), jnp.arange(rows * top), side="right").astype(jnp.int32)
    table = members.reshape(top, rows).T
    table = table[jax.random.permutation(jax.random.fold_in(own, 1), rows)]
    turn = jax.random.randint(jax.random.fold_in(own, 2), (rows, 1), 0, top)
    return jnp.take_along_axis(table, (jnp.arange(top)[None, :] + turn) % top, axis=1)


def portions_of(amount, total, most, skew, full):
    portions = [(1 << 20) // math.isqrt(rank ** skew) + 1 for rank in range(1, amount + 1)]
    largest = most if full else min(most, max(-(-total // amount), total * portions[0] // sum(portions)))
    least = 1 if total - largest >= amount - 1 else 0
    counts, rest = [largest] + [least] * (amount - 1), total - largest - least * (amount - 1)
    while rest > 0:
        free = [i for i in range(1, amount) if counts[i] < largest] or [i for i in range(1, amount) if counts[i] < most]
        mass, budget = sum([portions[i] for i in free]), rest
        for i in free:
            more = min(most - counts[i], max(1, budget * portions[i] // mass), rest)
            counts[i] = counts[i] + more
            rest = rest - more
    return np.array(counts)


def bell_draw(rng, dims, deviation, reach, pieces=(), kind=jnp.bfloat16):
    array = deviation * jax.random.normal(rng, dims, jnp.float32)
    if pieces:
        array = array * shard_levels(rng, dims, pieces, -0.22, 0.18)
    return jnp.clip(array, -reach, reach).astype(kind)


def setup_inputs(seed: int = 0) -> dict:
    seeds = jax.random.split(jax.random.key(seed), 8)
    tokens_x = bell_draw(seeds[0], (TOKENS, D), 1.0, 6.0, ((0, 128),))
    grad_out = bell_draw(seeds[1], (TOKENS, D), 1.0, 6.0, ((0, 128),))
    expert_ids_keys = jax.random.split(jax.random.fold_in(seeds[2], 1), TOKENS // TOK_DEV)
    expert_ids_turns = jax.random.permutation(jax.random.fold_in(seeds[2], 3), TOKENS // TOK_DEV)
    expert_ids = jax.vmap(lambda own, number: routed_block(jax.random.fold_in(seeds[2], 2), own, number, TOK_DEV, EXPERTS, TOP, CAP, 2))(expert_ids_keys, expert_ids_turns).reshape((TOKENS, TOP))
    probs = jnp.clip(0.049804688 + 0.2998047 * jax.random.uniform(seeds[3], (TOKENS, TOP), jnp.float32) ** shard_levels(seeds[3], (TOKENS, TOP), ((0, 128),), -0.2, 0.2), 0.049804688, 0.34960938).astype(jnp.bfloat16)
    w_gate = bell_draw(seeds[4], (EXPERTS, D, FF), D ** -0.5, 0.125, ((0, 128),))
    w_up = bell_draw(seeds[5], (EXPERTS, D, FF), D ** -0.5, 0.125, ((0, 128),))
    w_down = bell_draw(seeds[6], (EXPERTS, FF, D), FF ** -0.5, 0.21875, ((0, 128),))
    return {"tokens_x": tokens_x, "grad_out": grad_out, "expert_ids": expert_ids, "probs": probs, "w_gate": w_gate, "w_up": w_up, "w_down": w_down}


def expert_backward(rows_x, rows_dy, rows_p, gate_e, up_e, down_e):
    gate_pre = jnp.dot(rows_x, gate_e, preferred_element_type=jnp.float32)
    up_pre = jnp.dot(rows_x, up_e, preferred_element_type=jnp.float32)
    sigmoid_g = jax.nn.sigmoid(gate_pre)
    activated = gate_pre * sigmoid_g
    hidden_f = activated * up_pre
    hidden_grad = lax.dot_general(rows_dy, down_e, (((1,), (1,)), ((), ())), preferred_element_type=jnp.float32)
    prob_grad = jnp.sum(hidden_grad * hidden_f, axis=1).astype(jnp.bfloat16)
    weight_col = rows_p.astype(jnp.float32)[:, None]
    scaled_grad = hidden_grad * weight_col
    weighted_hidden = (hidden_f * weight_col).astype(jnp.bfloat16)
    up_rows = (scaled_grad * activated).astype(jnp.bfloat16)
    gate_rows = (scaled_grad * up_pre * sigmoid_g * (1.0 + gate_pre * (1.0 - sigmoid_g))).astype(jnp.bfloat16)
    input_grad = lax.dot_general(gate_rows, gate_e, (((1,), (1,)), ((), ())), preferred_element_type=jnp.float32)
    input_grad = input_grad + lax.dot_general(up_rows, up_e, (((1,), (1,)), ((), ())), preferred_element_type=jnp.float32)
    input_grad = input_grad.astype(jnp.bfloat16)
    gate_wgrad = lax.dot_general(rows_x, gate_rows, (((0,), (0,)), ((), ())), preferred_element_type=jnp.float32).astype(jnp.bfloat16)
    up_wgrad = lax.dot_general(rows_x, up_rows, (((0,), (0,)), ((), ())), preferred_element_type=jnp.float32).astype(jnp.bfloat16)
    down_wgrad = lax.dot_general(weighted_hidden, rows_dy, (((0,), (0,)), ((), ())), preferred_element_type=jnp.float32).astype(jnp.bfloat16)
    return input_grad, prob_grad, gate_wgrad, up_wgrad, down_wgrad


def reference(tokens_x, grad_out, expert_ids, probs, w_gate, w_up, w_down):
    devices = N_NODE * N_LOCAL
    per_device = TOK_DEV * TOP
    routed = expert_ids.reshape(devices, per_device).astype(jnp.int32)
    expert_row = jnp.arange(EXPERTS, dtype=jnp.int32)
    one_hot = (routed[:, :, None] == expert_row[None, None, :]).astype(jnp.int32)
    earlier = jnp.cumsum(one_hot, axis=1) - 1
    slot_index = jnp.sum(earlier * one_hot, axis=2).astype(jnp.int32)
    device_rows = jnp.broadcast_to(jnp.arange(devices, dtype=jnp.int32)[:, None], routed.shape)
    global_rows = device_rows * per_device + jnp.arange(per_device, dtype=jnp.int32)[None, :]
    table = jnp.full((devices, EXPERTS, CAP), TOKENS * TOP, jnp.int32)
    table = table.at[device_rows, routed, slot_index].set(global_rows)
    padded_x = jnp.concatenate([tokens_x, jnp.zeros((1, D), jnp.bfloat16)], axis=0)
    padded_dy = jnp.concatenate([grad_out, jnp.zeros((1, D), jnp.bfloat16)], axis=0)
    padded_p = jnp.concatenate([probs.reshape(-1), jnp.zeros((1,), jnp.bfloat16)], axis=0)

    def one_expert(carry, expert):
        input_acc, prob_acc = carry
        rows = table[:, expert, :].reshape(-1)
        token_rows = rows // TOP
        result = expert_backward(padded_x[token_rows], padded_dy[token_rows], padded_p[rows],
                                 w_gate[expert], w_up[expert], w_down[expert])
        input_acc = input_acc.at[token_rows].add(result[0].astype(jnp.float32))
        prob_acc = prob_acc.at[rows].add(result[1].astype(jnp.float32))
        return (input_acc, prob_acc), (result[2], result[3], result[4])

    start = (jnp.zeros((TOKENS + 1, D), jnp.float32), jnp.zeros((TOKENS * TOP + 1,), jnp.float32))
    (input_acc, prob_acc), grads = lax.scan(one_expert, start, jnp.arange(EXPERTS, dtype=jnp.int32))
    grad_x = input_acc[:TOKENS].astype(jnp.bfloat16)
    grad_probs = prob_acc[:TOKENS * TOP].reshape(TOKENS, TOP).astype(jnp.bfloat16)
    return grad_x, grad_probs, grads[0], grads[1], grads[2]
```

```python
import functools

import jax
import jax.numpy as jnp
import numpy as np
from jax import lax
from jax.experimental import pallas as pl
from jax.experimental.pallas import tpu as pltpu
from jax.sharding import PartitionSpec as P

MESH = pl.DeviceIdType.MESH
BF = jnp.bfloat16
F32 = jnp.float32
TOK, DIM, HID, TOP = 128, 2048, 768, 8
QW = 512
HW = QW // 2
AXES_X = (0, 1, 2, 0)
AXES_DY = (1, 2, 0, 1)
AXES_PART = (2, 0, 1, 2)
OTHERS = {0: (1, 2), 1: (0, 2), 2: (0, 1)}


def unfold_table():
    table = np.zeros((3, 2, 128, 256), np.float32)
    for source in range(128):
        co = (source // 32, (source // 8) % 4, (source // 2) % 4)
        core = source % 2
        for axis in range(3):
            o1, o2 = OTHERS[axis]
            plane = co[o1] * 4 + co[o2]
            for half in range(2):
                table[axis, half, source, plane * 16 + half * 8 + co[axis] * 2 + core] = 1
    return table


class Place:
    def __init__(self):
        node, local = lax.axis_index("node"), lax.axis_index("local")
        self.pos = (lax.rem(node, 4), lax.div(node, 4), lax.div(local, 2))
        self.core = lax.rem(local, 2)
        self.mate_core = 1 - self.core

    def dev(self, co, core):
        return (co[1] * 4 + co[0], co[2] * 2 + core)

    def on_axis(self, axis, value, core):
        co = list(self.pos)
        co[axis] = value
        return self.dev(co, core)

    def on_plane(self, axis, first, second):
        co = list(self.pos)
        co[OTHERS[axis][0]], co[OTHERS[axis][1]] = first, second
        return self.dev(co, self.core)

    def plane(self, axis):
        o1, o2 = OTHERS[axis]
        return self.pos[o1] * 4 + self.pos[o2]

    def mate(self):
        return self.dev(self.pos, self.mate_core)

    def line(self, axis):
        idx = list(self.pos)
        idx[axis] = pl.ds(0, 4)
        return tuple(idx)


def plane_peer(place, axis, step):
    o1, o2 = OTHERS[axis]
    first = lax.rem(place.pos[o1] + lax.rem(lax.rem(step, 4) + lax.div(step, 4), 4), 4)
    second = lax.rem(place.pos[o2] + lax.rem(step, 4), 4)
    return place.on_plane(axis, first, second), first * 4 + second


def remote(src, dst, send, recv, device):
    return pltpu.make_async_remote_copy(
        src_ref=src, dst_ref=dst, send_sem=send, recv_sem=recv, device_id=device, device_id_type=MESH
    )


def greet(place):
    barrier = pltpu.get_barrier_semaphore()

    def signal(device):
        pl.semaphore_signal(barrier, inc=1, device_id=device, device_id_type=MESH)

    count = 0
    for axis in range(3):
        for delta in range(1, 4):
            at = lax.rem(place.pos[axis] + delta, 4)
            signal(place.on_axis(axis, at, place.core))
            signal(place.on_axis(axis, at, place.mate_core))
            count += 2
        o1, o2 = OTHERS[axis]
        for d1 in range(1, 4):
            for d2 in range(1, 4):
                signal(place.on_plane(axis, lax.rem(place.pos[o1] + d1, 4), lax.rem(place.pos[o2] + d2, 4)))
                count += 1
    signal(place.mate())
    return count + 1


def await_greetings(count):
    pl.semaphore_wait(pltpu.get_barrier_semaphore(), count)


def build_select(rank_ref, weight_ref, axis, chip, main_ref, ninth_ref):
    row = lax.broadcasted_iota(jnp.int32, (16, 16, 128), 1)
    for core in range(2):
        at = axis * 8 + chip * 2 + core
        rank = jnp.broadcast_to(rank_ref[at][:, None, :], (16, 16, 128))
        if weight_ref is None:
            one = jnp.ones((16, 16, 128), F32)
        else:
            one = jnp.broadcast_to(weight_ref[at][:, None, :], (16, 16, 128))
        inside = (row < 8) if core == 0 else (row >= 8)
        lanes = pl.ds(core * 128, 128)
        main = jnp.where(inside & (rank == row - 8 * core), one, 0.0)
        main_ref[:, lanes] = main.reshape(256, 128).astype(BF)
        last = jnp.where(rank == 8, one, 0.0)
        for half in range(2):
            picked = jnp.where(row == half * 8 + chip * 2 + core, last, 0.0)
            ninth_ref[half, :, lanes] = picked.reshape(256, 128).astype(BF)


def dot(a, b, dims):
    return lax.dot_general(a, b, (dims, ((), ())), preferred_element_type=F32)


NN, NT, TN = ((1,), (0,)), ((1,), (1,)), ((0,), (0,))


def forward_kernel(
    x_ref, dy_ref, info_ref, table_ref, gate_hbm, up_hbm, down_hbm,
    xr_ref, x9_ref, dyr_ref, dy9_ref, h_ref, du_ref, dg_ref, gp_ref, rank_ref, infos_ref,
    gath, send, send9, recv9, weight_ref, main_sel, ninth_sel, gate, up, down, g_acc, u_acc, dh_acc, row_sum,
    w_sem, info_send, info_recv, g1_send, g1_recv, g2_send, g2_recv, p_send, p_recv, p9_send, p9_recv,
):
    place = Place()
    pos, core = place.pos, place.core
    loads = [
        pltpu.make_async_copy(src, dst, w_sem.at[i])
        for i, (src, dst) in enumerate(((gate_hbm, gate), (up_hbm, up), (down_hbm, down)))
    ]
    for load in loads:
        load.start()
    count = greet(place)
    tokens = (x_ref, dy_ref)
    axes = (AXES_X, AXES_DY)
    landing = (xr_ref, dyr_ref)
    landing9 = (x9_ref, dy9_ref)
    for axis in range(3):
        infos_ref[axis * 8 + pos[axis] * 2 + core] = info_ref[...]
    for arr in range(2):
        for q in range(4):
            gath[arr, q, pos[axes[arr][q]], core] = tokens[arr][:, q * QW:(q + 1) * QW]
    await_greetings(count)

    for axis in range(3):
        mine = infos_ref.at[axis * 8 + pos[axis] * 2 + core]
        for delta in range(4):
            at = lax.rem(pos[axis] + delta, 4)
            if delta:
                remote(info_ref, mine, info_send, info_recv, place.on_axis(axis, at, core)).start()
            remote(info_ref, mine, info_send, info_recv, place.on_axis(axis, at, place.mate_core)).start()

    def gather(arr):
        for delta in range(1, 4):
            for q in range(4):
                axis = axes[arr][q]
                mine = gath.at[arr, q, pos[axis], core]
                at = lax.rem(pos[axis] + delta, 4)
                remote(
                    mine, mine, g1_send.at[arr], g1_recv.at[arr, q, pos[axis]], place.on_axis(axis, at, core)
                ).start()

    def forward(arr, q):
        axis = axes[arr][q]
        for delta in range(4):
            at = lax.rem(pos[axis] + delta, 4)
            block = gath.at[arr, q, at, core]
            if delta:
                remote(block, block, g1_send.at[arr], g1_recv.at[arr, q, at], place.mate()).wait_recv()
            remote(block, block, g2_send.at[arr], g2_recv.at[arr, q, at], place.mate()).start()

    def select(arr, q):
        axis = axes[arr][q]
        for chip in range(4):
            build_select(rank_ref, weight_ref if arr else None, axis, chip, main_sel, ninth_sel)
            theirs = gath.at[arr, q, chip, place.mate_core]
            remote(theirs, theirs, g2_send.at[arr], g2_recv.at[arr, q, chip], place.mate()).wait_recv()
            block = gath[arr, q, chip].reshape(256, QW)
            rows = dot(main_sel[...], block, NN)
            send[arr, q, :, chip] = rows.reshape(16, 16, QW).astype(BF)
            last = dot(ninth_sel[0], block[:, :HW], NN) + dot(ninth_sel[1], block[:, HW:], NN)
            last = last.reshape(16, 16, HW).astype(BF)
            if chip:
                last = last + send9[arr, q]
            send9[arr, q] = last

    def scatter(arr, q):
        axis = axes[arr][q]
        me = place.plane(axis)
        target = landing[arr].at[(*place.line(axis), pl.ds(0, 16), pl.ds(q * QW, QW))]
        target9 = recv9.at[arr, q, me]
        sems = (p_send.at[arr, q], p_recv.at[arr, q])
        sems9 = (p9_send.at[arr, q], p9_recv.at[arr, q])

        def body(step, carry):
            device, index = plane_peer(place, axis, step)
            remote(send.at[arr, q, index], target, *sems, device).start()
            remote(send9.at[arr, q, index], target9, *sems9, device).start()
            return carry

        lax.fori_loop(1, 16, body, 0)
        pltpu.make_async_copy(send.at[arr, q, me], target, sems[1]).start()
        pltpu.make_async_copy(send9.at[arr, q, me], target9, sems9[1]).start()

    def arrive(arr, q):
        axis = axes[arr][q]
        whole = landing[arr].at[:, :, :, :, pl.ds(q * QW, QW)]
        pltpu.make_async_copy(whole, whole, p_recv.at[arr, q]).wait()
        whole = recv9.at[arr, q]
        pltpu.make_async_copy(whole, whole, p9_recv.at[arr, q]).wait()
        folded = recv9[arr, q].reshape(256, HW)
        for half in range(2):
            rows = dot(table_ref[axis, half], folded, NN).astype(BF)
            landing9[arr][:, q * QW + half * HW:q * QW + (half + 1) * HW] = rows

    gather(0)
    gather(1)

    whole = infos_ref.at[pl.ds(0, 21)]
    pltpu.make_async_copy(whole, whole, info_recv).wait()
    before = (
        lax.broadcasted_iota(jnp.int32, (128, 128), 0) < lax.broadcasted_iota(jnp.int32, (128, 128), 1)
    ).astype(F32).astype(BF)
    index = lax.broadcasted_iota(jnp.int32, (16, 128), 0)
    for axis in range(3):
        co = list(pos)
        o1, o2 = OTHERS[axis]
        co[o1], co[o2] = lax.shift_right_logical(index, 2), lax.bitwise_and(index, 3)
        expert = ((co[1] * 4 + co[0]) * 8 + co[2] * 2 + core).astype(F32)
        for at in range(axis * 8, axis * 8 + 8):
            info = infos_ref[at]
            chosen = jnp.zeros((16, 128), F32)
            weight = jnp.zeros((16, 128), F32)
            for k in range(TOP):
                hit = info[k:k + 1, :] == expert
                chosen = chosen + jnp.where(hit, 1.0, 0.0)
                weight = weight + jnp.where(hit, jnp.broadcast_to(info[8 + k:9 + k, :], (16, 128)), 0.0)
            rank = dot(chosen.astype(BF), before, NN)
            rank_ref[at] = jnp.where(chosen > 0.0, rank, -1.0).astype(jnp.int32)
            weight_ref[at] = weight

    for q in range(4):
        forward(0, q)
        select(0, q)
        scatter(0, q)
    for q in range(4):
        forward(1, q)
        select(1, q)
        scatter(1, q)
    for load in loads:
        load.wait()

    def accumulate(arr, q, outs):
        arrive(arr, q)

        def body(block, carry):
            lhs = landing[arr][block, :, :, :, q * QW:(q + 1) * QW].reshape(256, QW)
            for weights, dims, acc in outs:
                value = dot(lhs, weights, dims)
                if q:
                    value = value + acc[pl.ds(block * 256, 256), :]
                acc[pl.ds(block * 256, 256), :] = value
            return carry

        lax.fori_loop(0, 4, body, 0)
        lhs = landing9[arr][:, q * QW:(q + 1) * QW]
        for weights, dims, acc in outs:
            value = dot(lhs, weights, dims)
            if q:
                value = value + acc[1024:1152, :]
            acc[1024:1152, :] = value

    for q in range(4):
        rows = slice(q * QW, (q + 1) * QW)
        accumulate(0, q, ((gate[rows, :], NN, g_acc), (up[rows, :], NN, u_acc)))
    for q in range(4):
        rows = slice(q * QW, (q + 1) * QW)
        accumulate(1, q, ((down[:, rows], NT, dh_acc),))

    lane = lax.broadcasted_iota(jnp.int32, (16, 128), 1)
    slot = lax.bitwise_and(lax.broadcasted_iota(jnp.int32, (16, 128), 0), 7)

    def elementwise(step, carry):
        rows = pl.ds(step * 16, 16)
        g, u, dh = g_acc[rows, :], u_acc[rows, :], dh_acc[rows, :]
        s = 1.0 / (1.0 + jnp.exp(-g))
        a = g * s
        h = a * u
        h_ref[rows, :] = h.astype(BF)
        du_ref[rows, :] = (dh * a).astype(BF)
        dg_ref[rows, :] = (dh * u * s * (1.0 + g * (1.0 - s))).astype(BF)
        total = jnp.sum(dh * h, axis=1, keepdims=True)
        spread = jnp.where(step < 64, slot, 8)
        row_sum[rows, :] = jnp.where(lane == spread, total, 0.0)
        return carry

    lax.fori_loop(0, 72, elementwise, 0)
    gp_ref[...] = jnp.sum(row_sum[0:1024, :].reshape(128, 8, 128), axis=1) + row_sum[1024:1152, :]

    whole = infos_ref.at[pl.ds(0, 21)]
    pltpu.make_async_copy(whole, whole, info_send).wait()
    for arr in range(2):
        whole = gath.at[arr, :, pl.ds(0, 3), 0]
        pltpu.make_async_copy(whole, whole, g1_send.at[arr]).wait()
        whole = gath.at[arr, :, :, 0]
        pltpu.make_async_copy(whole, whole, g2_send.at[arr]).wait()
        for q in range(4):
            whole = send.at[arr, q, pl.ds(0, 15)]
            pltpu.make_async_copy(whole, whole, p_send.at[arr, q]).wait()
            whole = send9.at[arr, q, pl.ds(0, 15)]
            pltpu.make_async_copy(whole, whole, p9_send.at[arr, q]).wait()


def backward_kernel(
    xr_ref, x9_ref, dyr_ref, dy9_ref, h_ref, du_ref, dg_ref, gp_ref, rank_ref, infos_ref, table_ref, gate, up,
    gx_ref, gpt_ref, ggate_hbm, gup_hbm, gdown_hbm,
    send, send9, recv, recv9, main_sel, ninth_sel, own, mate_send, mate_recv, line_send, line_recv,
    gp_recv, gp_part, gp_back, stage, stage_d,
    p_send, p_recv, p9_send, p9_recv, m_send, m_recv, l_send, l_recv, gp_sems, gb_sems, out_sem,
):
    place = Place()
    pos, core = place.pos, place.core
    count = greet(place)

    def parts(q):
        axis = AXES_PART[q]
        cols = slice(q * QW, (q + 1) * QW)
        gate_q, up_q = gate[cols, :], up[cols, :]

        def body(block, carry):
            rows = pl.ds(block * 256, 256)
            value = dot(dg_ref[rows, :], gate_q, NT) + dot(du_ref[rows, :], up_q, NT)
            value = value.astype(BF).reshape(4, 4, 16, QW)
            if axis == 0:
                send[q, :, block] = value.reshape(16, 16, QW)
            elif axis == 1:
                for chip in range(4):
                    send[q, pl.ds(block * 4, 4), chip] = value[chip]
            else:
                send[q, pl.ds(block * 4, 4)] = value
            return carry

        lax.fori_loop(0, 4, body, 0)
        value = dot(dg_ref[1024:1152, :], gate_q, NT) + dot(du_ref[1024:1152, :], up_q, NT)
        value = value.astype(BF)
        folded = dot(table_ref[axis, 0], value[:, :HW], TN) + dot(table_ref[axis, 1], value[:, HW:], TN)
        send9[q] = folded.astype(BF).reshape(16, 16, HW)

    def scatter(q):
        axis = AXES_PART[q]
        me = place.plane(axis)

        def body(step, carry):
            device, index = plane_peer(place, axis, step)
            remote(send.at[q, index], recv.at[q, me], p_send.at[q], p_recv.at[q], device).start()
            remote(send9.at[q, index], recv9.at[q, me], p9_send.at[q], p9_recv.at[q], device).start()
            return carry

        lax.fori_loop(1, 16, body, 0)
        pltpu.make_async_copy(send.at[q, me], recv.at[q, me], p_recv.at[q]).start()
        pltpu.make_async_copy(send9.at[q, me], recv9.at[q, me], p9_recv.at[q]).start()

    parts(0)
    await_greetings(count)
    scatter(0)
    me_z = place.plane(2)

    def send_gp(step, carry):
        device, index = plane_peer(place, 2, step)
        remote(gp_ref.at[index], gp_recv.at[me_z], gp_sems.at[0], gp_sems.at[1], device).start()
        return carry

    lax.fori_loop(1, 16, send_gp, 0)
    pltpu.make_async_copy(gp_ref.at[me_z], gp_recv.at[me_z], gp_sems.at[1]).start()
    for q in range(1, 4):
        parts(q)
        scatter(q)

    def weight_grads(quarter):
        outs = []
        for piece in range(2):
            tile = quarter * 2 + piece
            cols = slice(tile * 256, (tile + 1) * 256)
            lhs = xr_ref[:, :, :, :, cols].reshape(1024, 256)
            lhs9 = x9_ref[:, cols]
            for which, (rows_ref, out) in enumerate(((dg_ref, ggate_hbm), (du_ref, gup_hbm))):
                slot = piece * 2 + which
                if quarter:
                    pltpu.make_async_copy(stage.at[slot], out.at[pl.ds(0, 256)], out_sem.at[slot]).wait()
                value = dot(lhs, rows_ref[0:1024, :], TN) + dot(lhs9, rows_ref[1024:1152, :], TN)
                stage[slot] = value.astype(BF)
                pltpu.make_async_copy(stage.at[slot], out.at[pl.ds(tile * 256, 256)], out_sem.at[slot]).start()
            rhs = dyr_ref[:, :, :, :, cols].reshape(1024, 256)
            if quarter:
                pltpu.make_async_copy(stage_d.at[piece], gdown_hbm.at[:, pl.ds(0, 256)], out_sem.at[4 + piece]).wait()
            value = dot(h_ref[0:1024, :], rhs, TN) + dot(h_ref[1024:1152, :], dy9_ref[:, cols], TN)
            stage_d[piece] = value.astype(BF)
            pltpu.make_async_copy(
                stage_d.at[piece], gdown_hbm.at[:, pl.ds(tile * 256, 256)], out_sem.at[4 + piece]
            ).start()

    def combine(q):
        axis = AXES_PART[q]
        whole = recv.at[q]
        pltpu.make_async_copy(whole, whole, p_recv.at[q]).wait()
        whole = recv9.at[q]
        pltpu.make_async_copy(whole, whole, p9_recv.at[q]).wait()
        last = recv9[q].reshape(256, HW)
        for chip in range(4):
            build_select(rank_ref, None, axis, chip, main_sel, ninth_sel)
            value = dot(main_sel[...], recv[q, :, chip].reshape(256, QW), TN)
            value = value + jnp.concatenate(
                [dot(ninth_sel[0], last, TN), dot(ninth_sel[1], last, TN)], axis=1
            )
            mine = core == 0
            own[q, chip] = jnp.where(mine, value[:128], value[128:])
            mate_send[q, chip] = jnp.where(mine, value[128:], value[:128]).astype(BF)
        remote(mate_send.at[q], mate_recv.at[q], m_send.at[q], m_recv.at[q], place.mate()).start()

    def to_line(q):
        axis = AXES_PART[q]
        remote(mate_send.at[q], mate_recv.at[q], m_send.at[q], m_recv.at[q], place.mate()).wait_recv()
        line_send[q] = (own[q] + mate_recv[q].astype(F32)).astype(BF)
        for delta in range(1, 4):
            at = lax.rem(pos[axis] + delta, 4)
            remote(
                line_send.at[q, at], line_recv.at[q, pos[axis]], l_send.at[q], l_recv.at[q],
                place.on_axis(axis, at, core),
            ).start()
        pltpu.make_async_copy(line_send.at[q, pos[axis]], line_recv.at[q, pos[axis]], l_recv.at[q]).start()

    def finish(q):
        whole = line_recv.at[q]
        pltpu.make_async_copy(whole, whole, l_recv.at[q]).wait()
        total = line_recv[q, 0].astype(F32) + line_recv[q, 1].astype(F32)
        total = total + line_recv[q, 2].astype(F32) + line_recv[q, 3].astype(F32)
        gx_ref[:, q * QW:(q + 1) * QW] = total.astype(BF)

    def probs_back():
        pltpu.make_async_copy(gp_recv, gp_recv, gp_sems.at[1]).wait()
        index = lax.broadcasted_iota(jnp.int32, (16, 128), 0)
        x, y = lax.shift_right_logical(index, 2), lax.bitwise_and(index, 3)
        expert = ((y * 4 + x) * 8 + pos[2] * 2 + core).astype(F32)
        for source in range(8):
            rank = rank_ref[16 + source]
            values = gp_recv[:, source, :]
            info = infos_ref[16 + source]
            spread = jnp.zeros((16, 128), F32)
            for j in range(9):
                spread = jnp.where(rank == j, values[:, j:j + 1], spread)
            for k in range(TOP):
                hit = info[k:k + 1, :] == expert
                gp_part[source, k:k + 1, :] = jnp.sum(jnp.where(hit, spread, 0.0), axis=0, keepdims=True)
        mine = pos[2] * 2 + core
        for delta in range(4):
            at = lax.rem(pos[2] + delta, 4)
            for whose in ((core, place.mate_core) if delta else (place.mate_core,)):
                remote(
                    gp_part.at[at * 2 + whose], gp_back.at[mine], gb_sems.at[0], gb_sems.at[1],
                    place.on_axis(2, at, whose),
                ).start()
        pltpu.make_async_copy(gp_part.at[mine], gp_back.at[mine], gb_sems.at[1]).start()

    weight_grads(0)
    weight_grads(1)
    probs_back()
    combine(0)
    weight_grads(2)
    to_line(0)
    combine(1)
    weight_grads(3)
    to_line(1)
    combine(2)
    finish(0)
    to_line(2)
    combine(3)
    finish(1)
    to_line(3)
    pltpu.make_async_copy(gp_back, gp_back, gb_sems.at[1]).wait()
    total = gp_back[0]
    for i in range(1, 8):
        total = total + gp_back[i]
    gpt_ref[...] = total
    finish(2)
    finish(3)

    for slot in range(4):
        pltpu.make_async_copy(stage.at[slot], ggate_hbm.at[pl.ds(0, 256)], out_sem.at[slot]).wait()
    for piece in range(2):
        pltpu.make_async_copy(stage_d.at[piece], gdown_hbm.at[:, pl.ds(0, 256)], out_sem.at[4 + piece]).wait()
    whole = gp_recv.at[pl.ds(0, 15)]
    pltpu.make_async_copy(whole, whole, gp_sems.at[0]).wait()
    whole = gp_back.at[pl.ds(0, 7)]
    pltpu.make_async_copy(whole, whole, gb_sems.at[0]).wait()
    for q in range(4):
        whole = send.at[q, pl.ds(0, 15)]
        pltpu.make_async_copy(whole, whole, p_send.at[q]).wait()
        whole = send9.at[q, pl.ds(0, 15)]
        pltpu.make_async_copy(whole, whole, p9_send.at[q]).wait()
        pltpu.make_async_copy(mate_send.at[q], mate_send.at[q], m_send.at[q]).wait()
        whole = line_send.at[q, pl.ds(0, 3)]
        pltpu.make_async_copy(whole, whole, l_send.at[q]).wait()


VMEM = pl.BlockSpec(memory_space=pltpu.VMEM)
ANY = pl.BlockSpec(memory_space=pl.ANY)
DMA = pltpu.SemaphoreType.DMA


def sds(*shape, dtype=BF):
    return jax.ShapeDtypeStruct(shape, dtype)


def shards(tokens_x, grad_out, expert_ids, probs, w_gate, w_up, w_down):
    info = jnp.concatenate([expert_ids.T.astype(F32), probs.T.astype(F32)], axis=0)
    table = jnp.asarray(unfold_table(), BF)
    gate, up, down = w_gate[0], w_up[0], w_down[0]
    (xr, x9, dyr, dy9, h, du, dg, gp, rank, infos) = pl.pallas_call(
        forward_kernel,
        out_shape=(
            sds(4, 4, 4, 16, DIM), sds(128, DIM), sds(4, 4, 4, 16, DIM), sds(128, DIM),
            sds(1152, HID), sds(1152, HID), sds(1152, HID), sds(128, 128, dtype=F32),
            sds(24, 16, 128, dtype=jnp.int32), sds(24, 16, 128, dtype=F32),
        ),
        in_specs=[VMEM] * 4 + [ANY] * 3,
        out_specs=(VMEM,) * 10,
        scratch_shapes=[
            pltpu.VMEM((2, 4, 4, 2, TOK, QW), BF),
            pltpu.VMEM((2, 4, 16, 4, 16, QW), BF),
            pltpu.VMEM((2, 4, 16, 16, HW), BF),
            pltpu.VMEM((2, 4, 16, 16, HW), BF),
            pltpu.VMEM((24, 16, 128), F32),
            pltpu.VMEM((256, 256), BF),
            pltpu.VMEM((2, 256, 256), BF),
            pltpu.VMEM((DIM, HID), BF),
            pltpu.VMEM((DIM, HID), BF),
            pltpu.VMEM((HID, DIM), BF),
            pltpu.VMEM((1152, HID), F32),
            pltpu.VMEM((1152, HID), F32),
            pltpu.VMEM((1152, HID), F32),
            pltpu.VMEM((1152, 128), F32),
            DMA((3,)), DMA, DMA, DMA((2,)), DMA((2, 4, 4)), DMA((2,)), DMA((2, 4, 4)),
            DMA((2, 4)), DMA((2, 4)), DMA((2, 4)), DMA((2, 4)),
        ],
        compiler_params=pltpu.CompilerParams(
            collective_id=1, has_side_effects=True, vmem_limit_bytes=60 << 20
        ),
        cost_estimate=pl.CostEstimate(flops=12 << 30, bytes_accessed=30 << 20, transcendentals=1 << 20),
    )(tokens_x, grad_out, info, table, gate, up, down)
    grad_x, gpt, grad_gate, grad_up, grad_down = pl.pallas_call(
        backward_kernel,
        out_shape=(
            sds(TOK, DIM), sds(TOP, TOK, dtype=F32), sds(DIM, HID), sds(DIM, HID), sds(HID, DIM),
        ),
        in_specs=[VMEM] * 13,
        out_specs=(VMEM, VMEM, ANY, ANY, ANY),
        scratch_shapes=[
            pltpu.VMEM((4, 16, 4, 16, QW), BF),
            pltpu.VMEM((4, 16, 16, HW), BF),
            pltpu.VMEM((4, 16, 4, 16, QW), BF),
            pltpu.VMEM((4, 16, 16, HW), BF),
            pltpu.VMEM((256, 256), BF),
            pltpu.VMEM((2, 256, 256), BF),
            pltpu.VMEM((4, 4, TOK, QW), F32),
            pltpu.VMEM((4, 4, TOK, QW), BF),
            pltpu.VMEM((4, 4, TOK, QW), BF),
            pltpu.VMEM((4, 4, TOK, QW), BF),
            pltpu.VMEM((4, 4, TOK, QW), BF),
            pltpu.VMEM((16, 8, 128), F32),
            pltpu.VMEM((8, 8, 128), F32),
            pltpu.VMEM((8, 8, 128), F32),
            pltpu.VMEM((4, 256, HID), BF),
            pltpu.VMEM((2, HID, 256), BF),
            DMA((4,)), DMA((4,)), DMA((4,)), DMA((4,)), DMA((4,)), DMA((4,)), DMA((4,)), DMA((4,)),
            DMA((2,)), DMA((2,)), DMA((6,)),
        ],
        compiler_params=pltpu.CompilerParams(
            collective_id=2, has_side_effects=True, vmem_limit_bytes=60 << 20
        ),
        cost_estimate=pl.CostEstimate(flops=18 << 30, bytes_accessed=30 << 20, transcendentals=0),
    )(xr, x9, dyr, dy9, h, du, dg, gp.reshape(16, 8, 128), rank, infos, table, gate, up)
    grad_probs = (gpt.T / probs.astype(F32)).astype(BF)
    return grad_x, grad_probs, grad_gate[None], grad_up[None], grad_down[None]


def solution(mesh):
    token = P(("node", "local"), None)
    weight = P(("node", "local"), None, None)
    return jax.shard_map(
        shards,
        mesh=mesh,
        in_specs=(token, token, token, token, weight, weight, weight),
        out_specs=(token, token, weight, weight, weight),
        check_vma=False,
    )
```

```python
import functools

import jax
import jax.numpy as jnp
import numpy as np
from jax import lax
from jax.experimental import pallas as pl
from jax.experimental.pallas import tpu as pltpu
from jax.sharding import PartitionSpec as P

MESH = pl.DeviceIdType.MESH
BF = jnp.bfloat16
F32 = jnp.float32
TOK, DIM, HID, TOP = 128, 2048, 768, 8
QW = 512
HW = QW // 2
AXES_X = (0, 1, 2, 0)
AXES_DY = (1, 2, 0, 1)
AXES_PART = (2, 0, 1, 2)
OTHERS = {0: (1, 2), 1: (0, 2), 2: (0, 1)}


def unfold_table():
    table = np.zeros((3, 2, 128, 256), np.float32)
    for source in range(128):
        co = (source // 32, (source // 8) % 4, (source // 2) % 4)
        core = source % 2
        for axis in range(3):
            o1, o2 = OTHERS[axis]
            plane = co[o1] * 4 + co[o2]
            for half in range(2):
                table[axis, half, source, plane * 16 + half * 8 + co[axis] * 2 + core] = 1
    return table


class Place:
    def __init__(self):
        node, local = lax.axis_index("node"), lax.axis_index("local")
        self.pos = (lax.rem(node, 4), lax.div(node, 4), lax.div(local, 2))
        self.core = lax.rem(local, 2)
        self.mate_core = 1 - self.core

    def dev(self, co, core):
        return (co[1] * 4 + co[0], co[2] * 2 + core)

    def on_axis(self, axis, value, core):
        co = list(self.pos)
        co[axis] = value
        return self.dev(co, core)

    def on_plane(self, axis, first, second):
        co = list(self.pos)
        co[OTHERS[axis][0]], co[OTHERS[axis][1]] = first, second
        return self.dev(co, self.core)

    def plane(self, axis):
        o1, o2 = OTHERS[axis]
        return self.pos[o1] * 4 + self.pos[o2]

    def mate(self):
        return self.dev(self.pos, self.mate_core)

    def line(self, axis):
        idx = list(self.pos)
        idx[axis] = pl.ds(0, 4)
        return tuple(idx)


def plane_peer(place, axis, step):
    o1, o2 = OTHERS[axis]
    first = lax.rem(place.pos[o1] + lax.rem(lax.rem(step, 4) + lax.div(step, 4), 4), 4)
    second = lax.rem(place.pos[o2] + lax.rem(step, 4), 4)
    return place.on_plane(axis, first, second), first * 4 + second


def remote(src, dst, send, recv, device):
    return pltpu.make_async_remote_copy(
        src_ref=src, dst_ref=dst, send_sem=send, recv_sem=recv, device_id=device, device_id_type=MESH
    )


def greet(place):
    barrier = pltpu.get_barrier_semaphore()

    def signal(device):
        pl.semaphore_signal(barrier, inc=1, device_id=device, device_id_type=MESH)

    count = 0
    for axis in range(3):
        for delta in range(1, 4):
            at = lax.rem(place.pos[axis] + delta, 4)
            signal(place.on_axis(axis, at, place.core))
            signal(place.on_axis(axis, at, place.mate_core))
            count += 2
        o1, o2 = OTHERS[axis]
        for d1 in range(1, 4):
            for d2 in range(1, 4):
                signal(place.on_plane(axis, lax.rem(place.pos[o1] + d1, 4), lax.rem(place.pos[o2] + d2, 4)))
                count += 1
    signal(place.mate())
    return count + 1


def await_greetings(count):
    pl.semaphore_wait(pltpu.get_barrier_semaphore(), count)


def build_select(rank_ref, weight_ref, axis, chip, main_ref, ninth_ref):
    row = lax.broadcasted_iota(jnp.int32, (16, 16, 128), 1)
    for core in range(2):
        at = axis * 8 + chip * 2 + core
        rank = jnp.broadcast_to(rank_ref[at][:, None, :], (16, 16, 128))
        if weight_ref is None:
            one = jnp.ones((16, 16, 128), F32)
        else:
            one = jnp.broadcast_to(weight_ref[at][:, None, :], (16, 16, 128))
        inside = (row < 8) if core == 0 else (row >= 8)
        lanes = pl.ds(core * 128, 128)
        main = jnp.where(inside & (rank == row - 8 * core), one, 0.0)
        main_ref[:, lanes] = main.reshape(256, 128).astype(BF)
        last = jnp.where(rank == 8, one, 0.0)
        for half in range(2):
            picked = jnp.where(row == half * 8 + chip * 2 + core, last, 0.0)
            ninth_ref[half, :, lanes] = picked.reshape(256, 128).astype(BF)


def dot(a, b, dims):
    return lax.dot_general(a, b, (dims, ((), ())), preferred_element_type=F32)


NN, NT, TN = ((1,), (0,)), ((1,), (1,)), ((0,), (0,))


def kernel(
    x_hbm, dy_hbm, info_ref, table_ref, gate_hbm, up_hbm, down_hbm,
    gx_ref, gpt_ref, ggate_hbm, gup_hbm, gdown_hbm,
    xr_ref, x9_ref, dyr_ref, dy9_ref, h_ref, du_ref, dg_ref, rank_ref, infos_ref, weight_ref,
    gath, send, send9, recv9, main_sel, ninth_sel, gate, up, down, g_acc, u_acc, dh_acc, row_sum,
    back, back9, mate_recv, line_recv, gp_ref, gp_recv, gp_part, gp_back,
    w_sem, info_send, info_recv, g1_send, g1_recv, g2_send, g2_recv, p_send, p_recv, p9_send, p9_recv,
    p_local, p9_local, m_send, m_recv, l_send, l_recv, gp_sems, gb_sems, out_sem,
):
    place = Place()
    pos, core = place.pos, place.core
    tokens = (x_hbm, dy_hbm)
    axes = (AXES_X, AXES_DY)
    landing = (xr_ref, dyr_ref)
    landing9 = (x9_ref, dy9_ref)
    for arr in range(2):
        for q in range(4):
            at = pos[axes[arr][q]]
            pltpu.make_async_copy(
                tokens[arr].at[:, pl.ds(q * QW, QW)], gath.at[arr, q, at, core], g1_recv.at[arr, q, at]
            ).start()
    loads = [
        pltpu.make_async_copy(src, dst, w_sem.at[i])
        for i, (src, dst) in enumerate(((gate_hbm, gate), (up_hbm, up), (down_hbm, down)))
    ]
    for load in loads:
        load.start()
    count = greet(place)
    for axis in range(3):
        infos_ref[axis * 8 + pos[axis] * 2 + core] = info_ref[...]
    await_greetings(count)

    for axis in range(3):
        mine = infos_ref.at[axis * 8 + pos[axis] * 2 + core]
        for delta in range(4):
            at = lax.rem(pos[axis] + delta, 4)
            if delta:
                remote(info_ref, mine, info_send, info_recv, place.on_axis(axis, at, core)).start()
            remote(info_ref, mine, info_send, info_recv, place.on_axis(axis, at, place.mate_core)).start()

    def gather(arr):
        for q in range(4):
            axis = axes[arr][q]
            for delta in (1, 3, 2):
                at = lax.rem(pos[axis] + delta, 4)
                remote(
                    tokens[arr].at[:, pl.ds(q * QW, QW)], gath.at[arr, q, pos[axis], core],
                    g1_send.at[arr], g1_recv.at[arr, q, pos[axis]], place.on_axis(axis, at, core),
                ).start()

    def forward(arr, q):
        axis = axes[arr][q]
        for delta in range(4):
            at = lax.rem(pos[axis] + delta, 4)
            block = gath.at[arr, q, at, core]
            pltpu.make_async_copy(block, block, g1_recv.at[arr, q, at]).wait()
            remote(block, block, g2_send.at[arr], g2_recv.at[arr, q, at], place.mate()).start()

    def select(arr, q):
        axis = axes[arr][q]
        for chip in range(4):
            build_select(rank_ref, weight_ref if arr else None, axis, chip, main_sel, ninth_sel)
            theirs = gath.at[arr, q, chip, place.mate_core]
            pltpu.make_async_copy(theirs, theirs, g2_recv.at[arr, q, chip]).wait()
            block = gath[arr, q, chip].reshape(256, QW)
            rows = dot(main_sel[...], block, NN)
            send[q, :, chip] = rows.reshape(16, 16, QW).astype(BF)
            last = dot(ninth_sel[0], block[:, :HW], NN) + dot(ninth_sel[1], block[:, HW:], NN)
            last = last.reshape(16, 16, HW).astype(BF)
            if chip:
                last = last + send9[q]
            send9[q] = last

    def scatter(arr, q):
        if arr < 2:
            axis = axes[arr][q]
            me = place.plane(axis)
            target = landing[arr].at[(*place.line(axis), pl.ds(0, 16), pl.ds(q * QW, QW))]
            target9 = recv9.at[arr, q, me]
        else:
            axis = AXES_PART[q]
            me = place.plane(axis)
            target = back.at[q, me]
            target9 = back9.at[q, me]
        sems = (p_send.at[arr, q], p_recv.at[arr, q])
        sems9 = (p9_send.at[arr, q], p9_recv.at[arr, q])

        def body(step, carry):
            device, index = plane_peer(place, axis, step)
            remote(send.at[q, index], target, *sems, device).start()
            remote(send9.at[q, index], target9, *sems9, device).start()
            return carry

        lax.fori_loop(1, 16, body, 0)
        pltpu.make_async_copy(send.at[q, me], target, p_local.at[arr, q]).start()
        pltpu.make_async_copy(send9.at[q, me], target9, p9_local.at[arr, q]).start()

    def sent(arr, q):
        whole = send.at[q, pl.ds(0, 15)]
        pltpu.make_async_copy(whole, whole, p_send.at[arr, q]).wait()
        whole = send9.at[q, pl.ds(0, 15)]
        pltpu.make_async_copy(whole, whole, p9_send.at[arr, q]).wait()

    def kept(arr, q):
        one = send.at[q, 0]
        pltpu.make_async_copy(one, one, p_local.at[arr, q]).wait()
        one = send9.at[q, 0]
        pltpu.make_async_copy(one, one, p9_local.at[arr, q]).wait()

    def received(arr, q):
        whole = send.at[q, pl.ds(0, 15)]
        pltpu.make_async_copy(whole, whole, p_recv.at[arr, q]).wait()
        whole = send9.at[q, pl.ds(0, 15)]
        pltpu.make_async_copy(whole, whole, p9_recv.at[arr, q]).wait()

    def arrive(arr, q):
        axis = axes[arr][q]
        received(arr, q)
        if arr:
            kept(arr, q)
        folded = recv9[arr, q].reshape(256, HW)
        for half in range(2):
            rows = dot(table_ref[axis, half], folded, NN).astype(BF)
            landing9[arr][:, q * QW + half * HW:q * QW + (half + 1) * HW] = rows

    gather(0)
    gather(1)

    whole = infos_ref.at[pl.ds(0, 21)]
    pltpu.make_async_copy(whole, whole, info_recv).wait()
    before = (
        lax.broadcasted_iota(jnp.int32, (128, 128), 0) < lax.broadcasted_iota(jnp.int32, (128, 128), 1)
    ).astype(F32).astype(BF)
    index = lax.broadcasted_iota(jnp.int32, (16, 128), 0)
    for axis in range(3):
        co = list(pos)
        o1, o2 = OTHERS[axis]
        co[o1], co[o2] = lax.shift_right_logical(index, 2), lax.bitwise_and(index, 3)
        expert = ((co[1] * 4 + co[0]) * 8 + co[2] * 2 + core).astype(F32)
        for at in range(axis * 8, axis * 8 + 8):
            info = infos_ref[at]
            chosen = jnp.zeros((16, 128), F32)
            weight = jnp.zeros((16, 128), F32)
            for k in range(TOP):
                hit = info[k:k + 1, :] == expert
                chosen = chosen + jnp.where(hit, 1.0, 0.0)
                weight = weight + jnp.where(hit, jnp.broadcast_to(info[8 + k:9 + k, :], (16, 128)), 0.0)
            rank = dot(chosen.astype(BF), before, NN)
            rank_ref[at] = jnp.where(chosen > 0.0, rank, -1.0).astype(jnp.int32)
            weight_ref[at] = weight

    def accumulate(arr, q, outs):
        arrive(arr, q)

        def body(block, carry):
            lhs = landing[arr][block, :, :, :, q * QW:(q + 1) * QW].reshape(256, QW)
            for weights, dims, acc in outs:
                value = dot(lhs, weights, dims)
                if q:
                    value = value + acc[pl.ds(block * 256, 256), :]
                acc[pl.ds(block * 256, 256), :] = value
            return carry

        lax.fori_loop(0, 4, body, 0)
        lhs = landing9[arr][:, q * QW:(q + 1) * QW]
        for weights, dims, acc in outs:
            value = dot(lhs, weights, dims)
            if q:
                value = value + acc[1024:1152, :]
            acc[1024:1152, :] = value

    for q in range(4):
        forward(0, q)
        select(0, q)
        scatter(0, q)
    for load in loads:
        load.wait()
    for q in range(4):
        forward(1, q)
        sent(0, q)
        kept(0, q)
        select(1, q)
        scatter(1, q)
        rows = slice(q * QW, (q + 1) * QW)
        accumulate(0, q, ((gate[rows, :], NN, g_acc), (up[rows, :], NN, u_acc)))

    def activations(step, carry):
        rows = pl.ds(step * 32, 32)
        g, u = g_acc[rows, :], u_acc[rows, :]
        s = 0.5 * jnp.tanh(0.5 * g) + 0.5
        a = g * s
        h_ref[rows, :] = (a * u).astype(BF)
        g_acc[rows, :] = a
        u_acc[rows, :] = u * (s + a * (1.0 - s))
        return carry

    lax.fori_loop(0, 36, activations, 0)
    for q in range(3):
        accumulate(1, q, ((down[:, q * QW:(q + 1) * QW], NT, dh_acc),))

    lane = lax.broadcasted_iota(jnp.int32, (32, 128), 1)
    slot = lax.bitwise_and(lax.broadcasted_iota(jnp.int32, (32, 128), 0), 7)

    def row_grads(step, carry):
        rows = pl.ds(step * 32, 32)
        dh = dh_acc[rows, :]
        du_ref[rows, :] = (dh * g_acc[rows, :]).astype(BF)
        dg_ref[rows, :] = (dh * u_acc[rows, :]).astype(BF)
        total = jnp.sum(dh * h_ref[rows, :].astype(F32), axis=1, keepdims=True)
        row_sum[rows, :] = jnp.where(lane == jnp.where(step < 32, slot, 8), total, 0.0)
        return carry

    def part_rows(rows, q):
        cols = slice(q * QW, (q + 1) * QW)
        value = dot(dg_ref[rows, :], gate[cols, :], NT) + dot(du_ref[rows, :], up[cols, :], NT)
        return value.astype(BF)

    def part_ninth(q):
        axis = AXES_PART[q]
        value = part_rows(slice(1024, 1152), q)
        folded = dot(table_ref[axis, 0], value[:, :HW], TN) + dot(table_ref[axis, 1], value[:, HW:], TN)
        send9[q] = folded.astype(BF).reshape(16, 16, HW)

    def part_block(q, block):
        axis = AXES_PART[q]
        value = part_rows(pl.ds(pl.multiple_of(block * 256, 256), 256), q).reshape(4, 4, 16, QW)
        if axis == 0:
            send[q, :, block] = value.reshape(16, 16, QW)
        elif axis == 1:
            for chip in range(4):
                send[q, pl.ds(block * 4, 4), chip] = value[chip]
        else:
            send[q, pl.ds(block * 4, 4)] = value

    arrive(1, 3)
    last = slice(3 * QW, 4 * QW)
    sent(1, 0)
    dh_acc[1024:1152, :] = dh_acc[1024:1152, :] + dot(dy9_ref[:, last], down[:, last], NT)
    lax.fori_loop(32, 36, row_grads, 0)
    part_ninth(0)
    me_z = place.plane(2)

    def first_back(step, carry):
        block = lax.rem(pos[0] + step, 4)
        rows = pl.ds(pl.multiple_of(block * 256, 256), 256)
        lhs = dyr_ref[block, :, :, :, last].reshape(256, QW)
        dh_acc[rows, :] = dh_acc[rows, :] + dot(lhs, down[:, last], NT)
        lax.fori_loop(block * 8, block * 8 + 8, row_grads, 0)
        part_block(0, block)
        for turn in range(4):
            second = lax.rem(pos[1] + turn, 4)
            index = block * 4 + second
            device = place.on_plane(2, block, second)

            def away():
                remote(send.at[0, index], back.at[0, me_z], p_send.at[2, 0], p_recv.at[2, 0], device).start()
                remote(send9.at[0, index], back9.at[0, me_z], p9_send.at[2, 0], p9_recv.at[2, 0], device).start()

            if turn == 0:
                @pl.when(step == 0)
                def _():
                    pltpu.make_async_copy(send.at[0, index], back.at[0, me_z], p_local.at[2, 0]).start()
                    pltpu.make_async_copy(send9.at[0, index], back9.at[0, me_z], p9_local.at[2, 0]).start()

                pl.when(step > 0)(away)
            else:
                away()
        return carry

    lax.fori_loop(0, 4, first_back, 0)
    sums = jnp.sum(row_sum[0:1024, :].reshape(128, 8, 128), axis=1) + row_sum[1024:1152, :]
    gp_ref[...] = sums.reshape(16, 8, 128)

    def send_gp(step, carry):
        device, index = plane_peer(place, 2, step)
        remote(gp_ref.at[index], gp_recv.at[me_z], gp_sems.at[0], gp_sems.at[1], device).start()
        return carry

    lax.fori_loop(1, 16, send_gp, 0)
    pltpu.make_async_copy(gp_ref.at[me_z], gp_recv.at[me_z], gp_sems.at[1]).start()

    def part_body(q):
        def body(block, carry):
            part_block(q, block)
            return carry

        return body

    for q in range(1, 4):
        sent(1, q)
        part_ninth(q)
        lax.fori_loop(0, 4, part_body(q), 0)
        scatter(2, q)

    whole = gath.at[0, :, :, 0]
    pltpu.make_async_copy(whole, whole, g2_send.at[0]).wait()

    def weight_grads(quarter):
        for tile in (quarter * 2, quarter * 2 + 1):
            cols = slice(tile * 256, (tile + 1) * 256)
            lhs = xr_ref[:, :, :, :, cols].reshape(1024, 256)
            lhs9 = x9_ref[:, cols]
            for which, (rows_ref, buffer, out) in enumerate(((dg_ref, gate, ggate_hbm), (du_ref, up, gup_hbm))):
                value = dot(lhs, rows_ref[0:1024, :], TN) + dot(lhs9, rows_ref[1024:1152, :], TN)
                buffer[cols, :] = value.astype(BF)
                pltpu.make_async_copy(buffer.at[cols], out.at[cols], out_sem.at[which]).start()
            rhs = dyr_ref[:, :, :, :, cols].reshape(1024, 256)
            value = dot(h_ref[0:1024, :], rhs, TN) + dot(h_ref[1024:1152, :], dy9_ref[:, cols], TN)
            down[:, cols] = value.astype(BF)
            pltpu.make_async_copy(down.at[:, cols], gdown_hbm.at[:, cols], out_sem.at[2]).start()

    def own(q, chip):
        return pl.ds(((q % 2) * 4 + chip) * 128, 128)

    def combine(q):
        axis = AXES_PART[q]
        received(2, q)
        kept(2, q)
        last = back9[q].reshape(256, HW)
        for chip in range(4):
            build_select(rank_ref, None, axis, chip, main_sel, ninth_sel)
            value = dot(main_sel[...], back[q, :, chip].reshape(256, QW), TN)
            value = value + jnp.concatenate(
                [dot(ninth_sel[0], last, TN), dot(ninth_sel[1], last, TN)], axis=1
            )
            mine = core == 0
            g_acc[own(q, chip), :QW] = jnp.where(mine, value[:128], value[128:])
            gath[0, q, chip, 0] = jnp.where(mine, value[128:], value[:128]).astype(BF)
        remote(gath.at[0, q, :, 0], mate_recv.at[q], m_send.at[q], m_recv.at[q], place.mate()).start()

    def to_line(q):
        axis = AXES_PART[q]
        whole = mate_recv.at[q]
        pltpu.make_async_copy(whole, whole, m_recv.at[q]).wait()
        for chip in range(4):
            gath[0, q, chip, 1] = (g_acc[own(q, chip), :QW] + mate_recv[q, chip].astype(F32)).astype(BF)
        for delta in (1, 3, 2):
            at = lax.rem(pos[axis] + delta, 4)
            remote(
                gath.at[0, q, at, 1], line_recv.at[q, pos[axis]], l_send.at[q], l_recv.at[q],
                place.on_axis(axis, at, core),
            ).start()
        pltpu.make_async_copy(gath.at[0, q, pos[axis], 1], line_recv.at[q, pos[axis]], l_recv.at[q]).start()

    def finish(q):
        whole = line_recv.at[q]
        pltpu.make_async_copy(whole, whole, l_recv.at[q]).wait()
        total = line_recv[q, 0].astype(F32) + line_recv[q, 1].astype(F32)
        total = total + line_recv[q, 2].astype(F32) + line_recv[q, 3].astype(F32)
        gx_ref[:, q * QW:(q + 1) * QW] = total.astype(BF)

    def probs_back():
        pltpu.make_async_copy(gp_recv, gp_recv, gp_sems.at[1]).wait()
        expert = ((index_y * 4 + index_x) * 8 + pos[2] * 2 + core).astype(F32)
        for source in range(8):
            rank = rank_ref[16 + source]
            values = gp_recv[:, source, :]
            info = infos_ref[16 + source]
            spread = jnp.zeros((16, 128), F32)
            for j in range(9):
                spread = jnp.where(rank == j, values[:, j:j + 1], spread)
            for k in range(TOP):
                hit = info[k:k + 1, :] == expert
                gp_part[source, k:k + 1, :] = jnp.sum(jnp.where(hit, spread, 0.0), axis=0, keepdims=True)
        mine = pos[2] * 2 + core
        for delta in range(4):
            at = lax.rem(pos[2] + delta, 4)
            for whose in ((core, place.mate_core) if delta else (place.mate_core,)):
                remote(
                    gp_part.at[at * 2 + whose], gp_back.at[mine], gb_sems.at[0], gb_sems.at[1],
                    place.on_axis(2, at, whose),
                ).start()
        pltpu.make_async_copy(gp_part.at[mine], gp_back.at[mine], gb_sems.at[1]).start()

    index_x, index_y = lax.shift_right_logical(index, 2), lax.bitwise_and(index, 3)
    weight_grads(0)
    probs_back()
    combine(0)
    weight_grads(1)
    to_line(0)
    combine(1)
    weight_grads(2)
    to_line(1)
    combine(2)
    finish(0)
    weight_grads(3)
    to_line(2)
    combine(3)
    finish(1)
    to_line(3)
    pltpu.make_async_copy(gp_back, gp_back, gb_sems.at[1]).wait()
    total = gp_back[0]
    for i in range(1, 8):
        total = total + gp_back[i]
    gpt_ref[...] = total
    finish(2)

    for which, (buffer, out) in enumerate(((gate, ggate_hbm), (up, gup_hbm), (down, gdown_hbm))):
        pltpu.make_async_copy(buffer, out, out_sem.at[which]).wait()
    whole = infos_ref.at[pl.ds(0, 21)]
    pltpu.make_async_copy(whole, whole, info_send).wait()
    for arr in range(2):
        whole = gath.at[arr, :, pl.ds(0, 3), 0]
        pltpu.make_async_copy(whole, whole, g1_send.at[arr]).wait()
    whole = gath.at[1, :, :, 0]
    pltpu.make_async_copy(whole, whole, g2_send.at[1]).wait()
    whole = gp_recv.at[pl.ds(0, 15)]
    pltpu.make_async_copy(whole, whole, gp_sems.at[0]).wait()
    whole = gp_back.at[pl.ds(0, 7)]
    pltpu.make_async_copy(whole, whole, gb_sems.at[0]).wait()
    for q in range(4):
        sent(2, q)
        whole = mate_recv.at[q]
        pltpu.make_async_copy(whole, whole, m_send.at[q]).wait()
        whole = line_recv.at[q, pl.ds(0, 3)]
        pltpu.make_async_copy(whole, whole, l_send.at[q]).wait()
    finish(3)


VMEM = pl.BlockSpec(memory_space=pltpu.VMEM)
ANY = pl.BlockSpec(memory_space=pl.ANY)
DMA = pltpu.SemaphoreType.DMA


def sds(*shape, dtype=BF):
    return jax.ShapeDtypeStruct(shape, dtype)


def shards(tokens_x, grad_out, expert_ids, probs, w_gate, w_up, w_down):
    info = jnp.concatenate([expert_ids.T.astype(F32), probs.T.astype(F32)], axis=0)
    table = jnp.asarray(unfold_table(), BF)
    grad_x, gpt, grad_gate, grad_up, grad_down = pl.pallas_call(
        kernel,
        out_shape=(
            sds(TOK, DIM), sds(TOP, TOK, dtype=F32), sds(DIM, HID), sds(DIM, HID), sds(HID, DIM),
        ),
        in_specs=[ANY, ANY, VMEM, VMEM, ANY, ANY, ANY],
        out_specs=(VMEM, VMEM, ANY, ANY, ANY),
        scratch_shapes=[
            pltpu.VMEM((4, 4, 4, 16, DIM), BF),
            pltpu.VMEM((128, DIM), BF),
            pltpu.VMEM((4, 4, 4, 16, DIM), BF),
            pltpu.VMEM((128, DIM), BF),
            pltpu.VMEM((1152, HID), BF),
            pltpu.VMEM((1152, HID), BF),
            pltpu.VMEM((1152, HID), BF),
            pltpu.VMEM((24, 16, 128), jnp.int32),
            pltpu.VMEM((24, 16, 128), F32),
            pltpu.VMEM((24, 16, 128), F32),
            pltpu.VMEM((2, 4, 4, 2, TOK, QW), BF),
            pltpu.VMEM((4, 16, 4, 16, QW), BF),
            pltpu.VMEM((4, 16, 16, HW), BF),
            pltpu.VMEM((2, 4, 16, 16, HW), BF),
            pltpu.VMEM((256, 256), BF),
            pltpu.VMEM((2, 256, 256), BF),
            pltpu.VMEM((DIM, HID), BF),
            pltpu.VMEM((DIM, HID), BF),
            pltpu.VMEM((HID, DIM), BF),
            pltpu.VMEM((1152, HID), F32),
            pltpu.VMEM((1152, HID), F32),
            pltpu.VMEM((1152, HID), F32),
            pltpu.VMEM((1152, 128), F32),
            pltpu.VMEM((4, 16, 4, 16, QW), BF),
            pltpu.VMEM((4, 16, 16, HW), BF),
            pltpu.VMEM((4, 4, TOK, QW), BF),
            pltpu.VMEM((4, 4, TOK, QW), BF),
            pltpu.VMEM((16, 8, 128), F32),
            pltpu.VMEM((16, 8, 128), F32),
            pltpu.VMEM((8, 8, 128), F32),
            pltpu.VMEM((8, 8, 128), F32),
            DMA((3,)), DMA, DMA, DMA((2,)), DMA((2, 4, 4)), DMA((2,)), DMA((2, 4, 4)),
            DMA((3, 4)), DMA((3, 4)), DMA((3, 4)), DMA((3, 4)),
            DMA((3, 4)), DMA((3, 4)), DMA((4,)), DMA((4,)), DMA((4,)), DMA((4,)), DMA((2,)), DMA((2,)), DMA((3,)),
        ],
        compiler_params=pltpu.CompilerParams(
            collective_id=1, has_side_effects=True, vmem_limit_bytes=62 << 20
        ),
        cost_estimate=pl.CostEstimate(flops=30 << 30, bytes_accessed=30 << 20, transcendentals=1 << 20),
    )(tokens_x, grad_out, info, table, w_gate[0], w_up[0], w_down[0])
    grad_probs = (gpt.T / probs.astype(F32)).astype(BF)
    return grad_x, grad_probs, grad_gate[None], grad_up[None], grad_down[None]


def solution(mesh):
    token = P(("node", "local"), None)
    weight = P(("node", "local"), None, None)
    return jax.shard_map(
        shards,
        mesh=mesh,
        in_specs=(token, token, token, token, weight, weight, weight),
        out_specs=(token, token, weight, weight, weight),
        check_vma=False,
    )
```

```python
import functools

import jax
import jax.numpy as jnp
import numpy as np
from jax import lax
from jax.experimental import pallas as pl
from jax.experimental.pallas import tpu as pltpu
from jax.sharding import PartitionSpec as P

MESH = pl.DeviceIdType.MESH
BF = jnp.bfloat16
F32 = jnp.float32
TOK, DIM, HID, TOP = 128, 2048, 768, 8
QW = 512
HW = QW // 2
AXES_X = (0, 1, 2, 0)
AXES_DY = (1, 2, 0, 1)
AXES_PART = (2, 0, 1, 2)
OTHERS = {0: (1, 2), 1: (0, 2), 2: (0, 1)}


def unfold_table():
    table = np.zeros((3, 2, 128, 256), np.float32)
    for source in range(128):
        co = (source // 32, (source // 8) % 4, (source // 2) % 4)
        core = source % 2
        for axis in range(3):
            o1, o2 = OTHERS[axis]
            plane = co[o1] * 4 + co[o2]
            for half in range(2):
                table[axis, half, source, plane * 16 + half * 8 + co[axis] * 2 + core] = 1
    return table


class Place:
    def __init__(self):
        node, local = lax.axis_index("node"), lax.axis_index("local")
        self.pos = (lax.rem(node, 4), lax.div(node, 4), lax.div(local, 2))
        self.core = lax.rem(local, 2)
        self.mate_core = 1 - self.core

    def dev(self, co, core):
        return (co[1] * 4 + co[0], co[2] * 2 + core)

    def on_axis(self, axis, value, core):
        co = list(self.pos)
        co[axis] = value
        return self.dev(co, core)

    def on_plane(self, axis, first, second):
        co = list(self.pos)
        co[OTHERS[axis][0]], co[OTHERS[axis][1]] = first, second
        return self.dev(co, self.core)

    def plane(self, axis):
        o1, o2 = OTHERS[axis]
        return self.pos[o1] * 4 + self.pos[o2]

    def mate(self):
        return self.dev(self.pos, self.mate_core)

    def line(self, axis):
        idx = list(self.pos)
        idx[axis] = pl.ds(0, 4)
        return tuple(idx)


def plane_peer(place, axis, step):
    o1, o2 = OTHERS[axis]
    sign = 1 + 2 * place.core
    first = lax.rem(place.pos[o1] + sign * (lax.rem(step, 4) + lax.div(step, 4)), 4)
    second = lax.rem(place.pos[o2] + sign * lax.rem(step, 4), 4)
    return place.on_plane(axis, first, second), first * 4 + second


def remote(src, dst, send, recv, device):
    return pltpu.make_async_remote_copy(
        src_ref=src, dst_ref=dst, send_sem=send, recv_sem=recv, device_id=device, device_id_type=MESH
    )


def greet(place):
    barrier = pltpu.get_barrier_semaphore()

    def signal(device):
        pl.semaphore_signal(barrier, inc=1, device_id=device, device_id_type=MESH)

    count = 0
    for axis in range(3):
        for delta in range(1, 4):
            at = lax.rem(place.pos[axis] + delta, 4)
            signal(place.on_axis(axis, at, place.core))
            signal(place.on_axis(axis, at, place.mate_core))
            count += 2
        o1, o2 = OTHERS[axis]
        for d1 in range(1, 4):
            for d2 in range(1, 4):
                signal(place.on_plane(axis, lax.rem(place.pos[o1] + d1, 4), lax.rem(place.pos[o2] + d2, 4)))
                count += 1
    signal(place.mate())
    return count + 1


def await_greetings(count):
    pl.semaphore_wait(pltpu.get_barrier_semaphore(), count)


def build_select(rank_ref, weight_ref, axis, chip, main_ref, ninth_ref):
    row = lax.broadcasted_iota(jnp.int32, (16, 16, 128), 1)
    for core in range(2):
        at = axis * 8 + chip * 2 + core
        rank = jnp.broadcast_to(rank_ref[at][:, None, :], (16, 16, 128))
        if weight_ref is None:
            one = jnp.ones((16, 16, 128), F32)
        else:
            one = jnp.broadcast_to(weight_ref[at][:, None, :], (16, 16, 128))
        inside = (row < 8) if core == 0 else (row >= 8)
        lanes = pl.ds(core * 128, 128)
        main = jnp.where(inside & (rank == row - 8 * core), one, 0.0)
        main_ref[:, lanes] = main.reshape(256, 128).astype(BF)
        last = jnp.where(rank == 8, one, 0.0)
        for half in range(2):
            picked = jnp.where(row == half * 8 + chip * 2 + core, last, 0.0)
            ninth_ref[half, :, lanes] = picked.reshape(256, 128).astype(BF)


def dot(a, b, dims):
    return lax.dot_general(a, b, (dims, ((), ())), preferred_element_type=F32)


NN, NT, TN = ((1,), (0,)), ((1,), (1,)), ((0,), (0,))


def kernel(
    x_hbm, dy_hbm, ids_ref, probs_ref, table_ref, gate_hbm, up_hbm, down_hbm,
    gx_ref, gpt_ref, ggate_hbm, gup_hbm, gdown_hbm,
    xr_ref, x9_ref, dyr_ref, dy9_ref, h_ref, du_ref, dg_ref, info_ref, rank_ref, infos_ref, weight_ref,
    gath, send, send9, recv9, main_sel, ninth_sel, gate, up, down, g_acc, u_acc, dh_acc, row_sum,
    back, back9, mate_recv, line_recv, gp_ref, gp_recv, gp_part, gp_back,
    w_sem, info_send, info_recv, g1_send, g1_recv, g2_send, g2_recv, p_send, p_recv, p9_send, p9_recv,
    p_local, p9_local, c_send, c_recv, c_local, mc_send, mc_recv, m_send, m_recv, l_send, l_recv, gp_sems, gb_sems, out_sem,
):
    place = Place()
    pos, core = place.pos, place.core
    tokens = (x_hbm, dy_hbm)
    axes = (AXES_X, AXES_DY)
    landing = (xr_ref, dyr_ref)
    landing9 = (x9_ref, dy9_ref)
    for arr in range(2):
        for q in range(4):
            at = pos[axes[arr][q]]
            pltpu.make_async_copy(
                tokens[arr].at[:, pl.ds(q * QW, QW)], gath.at[arr, q, at, core], g1_recv.at[arr, q, at]
            ).start()
    loads = [
        pltpu.make_async_copy(src, dst, w_sem.at[i])
        for i, (src, dst) in enumerate(((gate_hbm, gate), (up_hbm, up), (down_hbm, down)))
    ]
    for load in loads:
        load.start()
    count = greet(place)
    info_ref[0:8, :] = ids_ref[...].astype(F32)
    info_ref[8:16, :] = probs_ref[...].astype(F32)
    for axis in range(3):
        infos_ref[axis * 8 + pos[axis] * 2 + core] = info_ref[...]
    await_greetings(count)

    for axis in range(3):
        mine = infos_ref.at[axis * 8 + pos[axis] * 2 + core]
        for delta in range(4):
            at = lax.rem(pos[axis] + delta, 4)
            if delta:
                remote(info_ref, mine, info_send, info_recv, place.on_axis(axis, at, core)).start()
            remote(info_ref, mine, info_send, info_recv, place.on_axis(axis, at, place.mate_core)).start()

    def gather(arr):
        for q in range(4):
            axis = axes[arr][q]
            for delta in (1, 3, 2):
                at = lax.rem(pos[axis] + delta, 4)
                remote(
                    tokens[arr].at[:, pl.ds(q * QW, QW)], gath.at[arr, q, pos[axis], core],
                    g1_send.at[arr], g1_recv.at[arr, q, pos[axis]], place.on_axis(axis, at, core),
                ).start()

    def forward(arr, q):
        axis = axes[arr][q]
        for delta in range(4):
            at = lax.rem(pos[axis] + delta, 4)
            block = gath.at[arr, q, at, core]
            pltpu.make_async_copy(block, block, g1_recv.at[arr, q, at]).wait()
            remote(block, block, g2_send.at[arr], g2_recv.at[arr, q, at], place.mate()).start()

    def select(arr, q):
        axis = axes[arr][q]
        for chip in range(4):
            build_select(rank_ref, weight_ref if arr else None, axis, chip, main_sel, ninth_sel)
            theirs = gath.at[arr, q, chip, place.mate_core]
            pltpu.make_async_copy(theirs, theirs, g2_recv.at[arr, q, chip]).wait()
            block = gath[arr, q, chip].reshape(256, QW)
            rows = dot(main_sel[...], block, NN)
            send[q, :, chip] = rows.reshape(16, 16, QW).astype(BF)
            last = dot(ninth_sel[0], block[:, :HW], NN) + dot(ninth_sel[1], block[:, HW:], NN)
            last = last.reshape(16, 16, HW).astype(BF)
            if chip:
                last = last + send9[q]
            send9[q] = last

    def scatter(arr, q, main=True):
        if arr < 2:
            axis = axes[arr][q]
            me = place.plane(axis)
            target = landing[arr].at[(*place.line(axis), pl.ds(0, 16), pl.ds(q * QW, QW))]
            target9 = recv9.at[arr, q, me]
        else:
            axis = AXES_PART[q]
            me = place.plane(axis)
            target = back.at[q, me]
            target9 = back9.at[q, me]
        sems = (p_send.at[arr, q], p_recv.at[arr, q])
        sems9 = (p9_send.at[arr, q], p9_recv.at[arr, q])

        def body(step, carry):
            device, index = plane_peer(place, axis, step)
            if main:
                remote(send.at[q, index], target, *sems, device).start()
            remote(send9.at[q, index], target9, *sems9, device).start()
            return carry

        lax.fori_loop(1, 16, body, 0)
        if main:
            pltpu.make_async_copy(send.at[q, me], target, p_local.at[arr, q]).start()
        pltpu.make_async_copy(send9.at[q, me], target9, p9_local.at[arr, q]).start()

    def sent(arr, q):
        whole = send.at[q, pl.ds(0, 15)]
        pltpu.make_async_copy(whole, whole, p_send.at[arr, q]).wait()
        whole = send9.at[q, pl.ds(0, 15)]
        pltpu.make_async_copy(whole, whole, p9_send.at[arr, q]).wait()

    def received9(arr, q):
        whole = send9.at[q, pl.ds(0, 15)]
        pltpu.make_async_copy(whole, whole, p9_recv.at[arr, q]).wait()
        one = send9.at[q, 0]
        pltpu.make_async_copy(one, one, p9_local.at[arr, q]).wait()

    def kept(arr, q):
        one = send.at[q, 0]
        pltpu.make_async_copy(one, one, p_local.at[arr, q]).wait()
        one = send9.at[q, 0]
        pltpu.make_async_copy(one, one, p9_local.at[arr, q]).wait()

    def received(arr, q):
        whole = send.at[q, pl.ds(0, 15)]
        pltpu.make_async_copy(whole, whole, p_recv.at[arr, q]).wait()
        whole = send9.at[q, pl.ds(0, 15)]
        pltpu.make_async_copy(whole, whole, p9_recv.at[arr, q]).wait()

    def unfold(arr, q):
        axis = axes[arr][q]
        folded = recv9[arr, q].reshape(256, HW)
        for half in range(2):
            rows = dot(table_ref[axis, half], folded, NN).astype(BF)
            landing9[arr][:, q * QW + half * HW:q * QW + (half + 1) * HW] = rows

    def arrive(arr, q):
        received(arr, q)
        if arr:
            kept(arr, q)
        unfold(arr, q)

    gather(0)
    gather(1)

    whole = infos_ref.at[pl.ds(0, 21)]
    pltpu.make_async_copy(whole, whole, info_recv).wait()
    before = (
        lax.broadcasted_iota(jnp.int32, (128, 128), 0) < lax.broadcasted_iota(jnp.int32, (128, 128), 1)
    ).astype(F32).astype(BF)
    index = lax.broadcasted_iota(jnp.int32, (16, 128), 0)
    for axis in range(3):
        co = list(pos)
        o1, o2 = OTHERS[axis]
        co[o1], co[o2] = lax.shift_right_logical(index, 2), lax.bitwise_and(index, 3)
        expert = ((co[1] * 4 + co[0]) * 8 + co[2] * 2 + core).astype(F32)
        for at in range(axis * 8, axis * 8 + 8):
            info = infos_ref[at]
            chosen = jnp.zeros((16, 128), F32)
            weight = jnp.zeros((16, 128), F32)
            for k in range(TOP):
                hit = info[k:k + 1, :] == expert
                chosen = chosen + jnp.where(hit, 1.0, 0.0)
                weight = weight + jnp.where(hit, jnp.broadcast_to(info[8 + k:9 + k, :], (16, 128)), 0.0)
            rank = dot(chosen.astype(BF), before, NN)
            rank_ref[at] = jnp.where(chosen > 0.0, rank, -1.0).astype(jnp.int32)
            weight_ref[at] = weight

    def accumulate(arr, q, outs):
        arrive(arr, q)

        def body(block, carry):
            lhs = landing[arr][block, :, :, :, q * QW:(q + 1) * QW].reshape(256, QW)
            for weights, dims, acc in outs:
                value = dot(lhs, weights, dims)
                if q:
                    value = value + acc[pl.ds(block * 256, 256), :]
                acc[pl.ds(block * 256, 256), :] = value
            return carry

        lax.fori_loop(0, 4, body, 0)
        lhs = landing9[arr][:, q * QW:(q + 1) * QW]
        for weights, dims, acc in outs:
            value = dot(lhs, weights, dims)
            if q:
                value = value + acc[1024:1152, :]
            acc[1024:1152, :] = value

    for q in range(4):
        forward(0, q)
        select(0, q)
        scatter(0, q)
    for load in loads:
        load.wait()
    for q in range(4):
        forward(1, q)
        sent(0, q)
        kept(0, q)
        select(1, q)
        scatter(1, q)
        rows = slice(q * QW, (q + 1) * QW)
        accumulate(0, q, ((gate[rows, :], NN, g_acc), (up[rows, :], NN, u_acc)))

    def activations(step, carry):
        rows = pl.ds(step * 32, 32)
        g, u = g_acc[rows, :], u_acc[rows, :]
        s = 0.5 * jnp.tanh(0.5 * g) + 0.5
        a = g * s
        h_ref[rows, :] = (a * u).astype(BF)
        g_acc[rows, :] = a
        u_acc[rows, :] = u * (s + a * (1.0 - s))
        return carry

    lax.fori_loop(0, 36, activations, 0)
    for q in range(3):
        accumulate(1, q, ((down[:, q * QW:(q + 1) * QW], NT, dh_acc),))

    lane = lax.broadcasted_iota(jnp.int32, (32, 128), 1)
    slot = lax.bitwise_and(lax.broadcasted_iota(jnp.int32, (32, 128), 0), 7)

    def row_grads(step, carry):
        rows = pl.ds(step * 32, 32)
        dh = dh_acc[rows, :]
        du_ref[rows, :] = (dh * g_acc[rows, :]).astype(BF)
        dg_ref[rows, :] = (dh * u_acc[rows, :]).astype(BF)
        total = jnp.sum(dh * h_ref[rows, :].astype(F32), axis=1, keepdims=True)
        row_sum[rows, :] = jnp.where(lane == jnp.where(step < 32, slot, 8), total, 0.0)
        return carry

    def part_rows(rows, q):
        cols = slice(q * QW, (q + 1) * QW)
        value = dot(dg_ref[rows, :], gate[cols, :], NT) + dot(du_ref[rows, :], up[cols, :], NT)
        return value.astype(BF)

    def part_ninth(q):
        axis = AXES_PART[q]
        value = part_rows(slice(1024, 1152), q)
        folded = dot(table_ref[axis, 0], value[:, :HW], TN) + dot(table_ref[axis, 1], value[:, HW:], TN)
        send9[q] = folded.astype(BF).reshape(16, 16, HW)

    def part_block(q, block):
        axis = AXES_PART[q]
        value = part_rows(pl.ds(pl.multiple_of(block * 256, 256), 256), q).reshape(4, 4, 16, QW)
        if axis == 0:
            send[q, :, block] = value.reshape(16, 16, QW)
        elif axis == 1:
            for chip in range(4):
                send[q, pl.ds(block * 4, 4), chip] = value[chip]
        else:
            send[q, pl.ds(block * 4, 4)] = value

    last = slice(3 * QW, 4 * QW)
    sent(1, 0)
    received(1, 3)
    kept(1, 3)
    me_z = place.plane(2)

    def first_back(step, carry):
        block = lax.rem(pos[0] + step, 4)
        rows = pl.ds(pl.multiple_of(block * 256, 256), 256)
        lhs = dyr_ref[block, :, :, :, last].reshape(256, QW)
        dh_acc[rows, :] = dh_acc[rows, :] + dot(lhs, down[:, last], NT)
        lax.fori_loop(block * 8, block * 8 + 8, row_grads, 0)
        part_block(0, block)
        for turn in range(4):
            second = lax.rem(pos[1] + turn, 4)
            index = block * 4 + second
            device = place.on_plane(2, block, second)

            def away():
                remote(send.at[0, index], back.at[0, me_z], p_send.at[2, 0], p_recv.at[2, 0], device).start()

            if turn == 0:
                @pl.when(step == 0)
                def _():
                    pltpu.make_async_copy(send.at[0, index], back.at[0, me_z], p_local.at[2, 0]).start()

                pl.when(step > 0)(away)
            else:
                away()
        return carry

    lax.fori_loop(0, 4, first_back, 0)
    unfold(1, 3)
    dh_acc[1024:1152, :] = dh_acc[1024:1152, :] + dot(dy9_ref[:, last], down[:, last], NT)
    lax.fori_loop(32, 36, row_grads, 0)
    part_ninth(0)
    scatter(2, 0, main=False)
    sums = jnp.sum(row_sum[0:1024, :].reshape(128, 8, 128), axis=1) + row_sum[1024:1152, :]
    gp_ref[...] = sums.reshape(16, 8, 128)

    def send_gp(step, carry):
        device, index = plane_peer(place, 2, step)
        remote(gp_ref.at[index], gp_recv.at[me_z], gp_sems.at[0], gp_sems.at[1], device).start()
        return carry

    lax.fori_loop(1, 16, send_gp, 0)
    pltpu.make_async_copy(gp_ref.at[me_z], gp_recv.at[me_z], gp_sems.at[1]).start()

    def part_body(q):
        def body(block, carry):
            part_block(q, block)
            return carry

        return body

    for q in range(1, 4):
        sent(1, q)
        part_ninth(q)
        lax.fori_loop(0, 4, part_body(q), 0)
        scatter(2, q, main=q < 3)

    line_chips = [lax.rem(pos[AXES_PART[3]] + delta, 4) for delta in (2, 1, 3, 0)]
    me_last = place.plane(AXES_PART[3])
    for turn, chip in enumerate(line_chips):
        def chip_away(step, carry):
            device, index = plane_peer(place, AXES_PART[3], step)
            remote(
                send.at[3, index, chip], back.at[3, me_last, chip], c_send.at[turn], c_recv.at[turn], device
            ).start()
            return carry

        lax.fori_loop(1, 16, chip_away, 0)
        pltpu.make_async_copy(send.at[3, me_last, chip], back.at[3, me_last, chip], c_local.at[turn]).start()

    whole = gath.at[0, :, :, 0]
    pltpu.make_async_copy(whole, whole, g2_send.at[0]).wait()

    def weight_grads(quarter):
        for tile in (quarter * 2, quarter * 2 + 1):
            cols = slice(tile * 256, (tile + 1) * 256)
            lhs = xr_ref[:, :, :, :, cols].reshape(1024, 256)
            lhs9 = x9_ref[:, cols]
            for which, (rows_ref, buffer, out) in enumerate(((dg_ref, gate, ggate_hbm), (du_ref, up, gup_hbm))):
                value = dot(lhs, rows_ref[0:1024, :], TN) + dot(lhs9, rows_ref[1024:1152, :], TN)
                buffer[cols, :] = value.astype(BF)
                pltpu.make_async_copy(buffer.at[cols], out.at[cols], out_sem.at[which]).start()
            rhs = dyr_ref[:, :, :, :, cols].reshape(1024, 256)
            value = dot(h_ref[0:1024, :], rhs, TN) + dot(h_ref[1024:1152, :], dy9_ref[:, cols], TN)
            down[:, cols] = value.astype(BF)
            pltpu.make_async_copy(down.at[:, cols], gdown_hbm.at[:, cols], out_sem.at[2]).start()

    def own(q, chip):
        return pl.ds(pl.multiple_of(((q % 2) * 4 + chip) * 128, 128), 128)

    def combine_chip(q, chip, ready=None):
        build_select(rank_ref, None, AXES_PART[q], chip, main_sel, ninth_sel)
        if ready is not None:
            ready()
        last = back9[q].reshape(256, HW)
        value = dot(main_sel[...], back[q, :, chip].reshape(256, QW), TN)
        value = value + jnp.concatenate([dot(ninth_sel[0], last, TN), dot(ninth_sel[1], last, TN)], axis=1)
        mine = core == 0
        g_acc[own(q, chip), :QW] = jnp.where(mine, value[:128], value[128:])
        gath[0, q, chip, 0] = jnp.where(mine, value[128:], value[:128]).astype(BF)

    def combine(q):
        received(2, q)
        kept(2, q)
        for chip in range(4):
            combine_chip(q, chip)
        remote(gath.at[0, q, :, 0], mate_recv.at[q], m_send.at[q], m_recv.at[q], place.mate()).start()

    def to_line(q):
        axis = AXES_PART[q]
        whole = mate_recv.at[q]
        pltpu.make_async_copy(whole, whole, m_recv.at[q]).wait()
        for chip in range(4):
            gath[0, q, chip, 1] = (g_acc[own(q, chip), :QW] + mate_recv[q, chip].astype(F32)).astype(BF)
        for delta in (1, 3, 2):
            at = lax.rem(pos[axis] + delta, 4)
            remote(
                gath.at[0, q, at, 1], line_recv.at[q, pos[axis]], l_send.at[q], l_recv.at[q],
                place.on_axis(axis, at, core),
            ).start()
        pltpu.make_async_copy(gath.at[0, q, pos[axis], 1], line_recv.at[q, pos[axis]], l_recv.at[q]).start()

    def combine_last(turn):
        chip = line_chips[turn]

        def ready():
            whole = send.at[3, pl.ds(0, 15), 0]
            pltpu.make_async_copy(whole, whole, c_recv.at[turn]).wait()
            one = send.at[3, 0, 0]
            pltpu.make_async_copy(one, one, c_local.at[turn]).wait()

        combine_chip(3, chip, ready)
        remote(
            gath.at[0, 3, chip, 0], mate_recv.at[3, chip], mc_send.at[turn], mc_recv.at[turn], place.mate()
        ).start()

    def line_last(turn):
        chip = line_chips[turn]
        one = mate_recv.at[3, chip]
        pltpu.make_async_copy(one, one, mc_recv.at[turn]).wait()
        gath[0, 3, chip, 1] = (g_acc[own(3, chip), :QW] + mate_recv[3, chip].astype(F32)).astype(BF)
        here = line_recv.at[3, pos[AXES_PART[3]]]
        if turn < 3:
            device = place.on_axis(AXES_PART[3], chip, core)
            remote(gath.at[0, 3, chip, 1], here, l_send.at[3], l_recv.at[3], device).start()
        else:
            pltpu.make_async_copy(gath.at[0, 3, chip, 1], here, l_recv.at[3]).start()

    def finish(q):
        whole = line_recv.at[q]
        pltpu.make_async_copy(whole, whole, l_recv.at[q]).wait()
        total = line_recv[q, 0].astype(F32) + line_recv[q, 1].astype(F32)
        total = total + line_recv[q, 2].astype(F32) + line_recv[q, 3].astype(F32)
        gx_ref[:, q * QW:(q + 1) * QW] = total.astype(BF)

    def probs_back():
        pltpu.make_async_copy(gp_recv, gp_recv, gp_sems.at[1]).wait()
        expert = ((index_y * 4 + index_x) * 8 + pos[2] * 2 + core).astype(F32)
        for source in range(8):
            rank = rank_ref[16 + source]
            values = gp_recv[:, source, :]
            info = infos_ref[16 + source]
            spread = jnp.zeros((16, 128), F32)
            for j in range(9):
                spread = jnp.where(rank == j, values[:, j:j + 1], spread)
            for k in range(TOP):
                hit = info[k:k + 1, :] == expert
                gp_part[source, k:k + 1, :] = jnp.sum(jnp.where(hit, spread, 0.0), axis=0, keepdims=True)
        mine = pos[2] * 2 + core
        for delta in range(4):
            at = lax.rem(pos[2] + delta, 4)
            for whose in ((core, place.mate_core) if delta else (place.mate_core,)):
                remote(
                    gp_part.at[at * 2 + whose], gp_back.at[mine], gb_sems.at[0], gb_sems.at[1],
                    place.on_axis(2, at, whose),
                ).start()
        pltpu.make_async_copy(gp_part.at[mine], gp_back.at[mine], gb_sems.at[1]).start()

    index_x, index_y = lax.shift_right_logical(index, 2), lax.bitwise_and(index, 3)
    weight_grads(0)
    probs_back()
    combine(0)
    weight_grads(1)
    to_line(0)
    combine(1)
    weight_grads(2)
    to_line(1)
    combine(2)
    finish(0)
    weight_grads(3)
    to_line(2)
    finish(1)
    received9(2, 3)
    combine_last(0)
    combine_last(1)
    line_last(0)
    combine_last(2)
    line_last(1)
    combine_last(3)
    line_last(2)
    line_last(3)
    pltpu.make_async_copy(gp_back, gp_back, gb_sems.at[1]).wait()
    total = gp_back[0]
    for i in range(1, 8):
        total = total + gp_back[i]
    gpt_ref[...] = total
    finish(2)

    for which, (buffer, out) in enumerate(((gate, ggate_hbm), (up, gup_hbm), (down, gdown_hbm))):
        pltpu.make_async_copy(buffer, out, out_sem.at[which]).wait()
    whole = infos_ref.at[pl.ds(0, 21)]
    pltpu.make_async_copy(whole, whole, info_send).wait()
    for arr in range(2):
        whole = gath.at[arr, :, pl.ds(0, 3), 0]
        pltpu.make_async_copy(whole, whole, g1_send.at[arr]).wait()
    whole = gath.at[1, :, :, 0]
    pltpu.make_async_copy(whole, whole, g2_send.at[1]).wait()
    whole = gp_recv.at[pl.ds(0, 15)]
    pltpu.make_async_copy(whole, whole, gp_sems.at[0]).wait()
    whole = gp_back.at[pl.ds(0, 7)]
    pltpu.make_async_copy(whole, whole, gb_sems.at[0]).wait()
    for q in range(3):
        sent(2, q)
        whole = mate_recv.at[q]
        pltpu.make_async_copy(whole, whole, m_send.at[q]).wait()
    whole = send9.at[3, pl.ds(0, 15)]
    pltpu.make_async_copy(whole, whole, p9_send.at[2, 3]).wait()
    for turn in range(4):
        whole = send.at[3, pl.ds(0, 15), 0]
        pltpu.make_async_copy(whole, whole, c_send.at[turn]).wait()
        one = mate_recv.at[3, 0]
        pltpu.make_async_copy(one, one, mc_send.at[turn]).wait()
    for q in range(4):
        whole = line_recv.at[q, pl.ds(0, 3)]
        pltpu.make_async_copy(whole, whole, l_send.at[q]).wait()
    finish(3)


def hand_over(
    gx_ref, gpt_ref, probs_ref, gate_ref, up_ref, down_ref, gx_out, probs_out, gate_out, up_out, down_out,
    gx, gate, up, down, in_sems, out_sems,
):
    steps = []
    for src, via, dst in (
        (gate_ref, gate, gate_out), (up_ref, up, up_out), (down_ref, down, down_out), (gx_ref, gx, gx_out)
    ):
        rows = max(src.shape[0] // 4, 128)
        for start in range(0, src.shape[0], rows):
            part, n = pl.ds(start, rows), len(steps)
            steps.append((
                pltpu.make_async_copy(src.at[part], via.at[part], in_sems.at[n]),
                pltpu.make_async_copy(via.at[part], dst.at[part], out_sems.at[n]),
            ))
    for load, _ in steps:
        load.start()
    probs_out[...] = (gpt_ref[...] / probs_ref[...].astype(F32)).astype(BF)
    for load, store in steps:
        load.wait()
        store.start()
    for _, store in steps:
        store.wait()


VMEM = pl.BlockSpec(memory_space=pltpu.VMEM)
ANY = pl.BlockSpec(memory_space=pl.ANY)
DMA = pltpu.SemaphoreType.DMA


def sds(*shape, dtype=BF):
    return jax.ShapeDtypeStruct(shape, dtype)


def shards(tokens_x, grad_out, expert_ids, probs, w_gate, w_up, w_down):
    ids_t, probs_t = expert_ids.T, probs.T
    table = jnp.asarray(unfold_table(), BF)
    grad_x, gpt, grad_gate, grad_up, grad_down = pl.pallas_call(
        kernel,
        out_shape=(
            sds(TOK, DIM), sds(TOP, TOK, dtype=F32), sds(DIM, HID), sds(DIM, HID), sds(HID, DIM),
        ),
        in_specs=[ANY, ANY, VMEM, VMEM, VMEM, ANY, ANY, ANY],
        out_specs=(VMEM, VMEM, ANY, ANY, ANY),
        scratch_shapes=[
            pltpu.VMEM((4, 4, 4, 16, DIM), BF),
            pltpu.VMEM((128, DIM), BF),
            pltpu.VMEM((4, 4, 4, 16, DIM), BF),
            pltpu.VMEM((128, DIM), BF),
            pltpu.VMEM((1152, HID), BF),
            pltpu.VMEM((1152, HID), BF),
            pltpu.VMEM((1152, HID), BF),
            pltpu.VMEM((16, 128), F32),
            pltpu.VMEM((24, 16, 128), jnp.int32),
            pltpu.VMEM((24, 16, 128), F32),
            pltpu.VMEM((24, 16, 128), F32),
            pltpu.VMEM((2, 4, 4, 2, TOK, QW), BF),
            pltpu.VMEM((4, 16, 4, 16, QW), BF),
            pltpu.VMEM((4, 16, 16, HW), BF),
            pltpu.VMEM((2, 4, 16, 16, HW), BF),
            pltpu.VMEM((256, 256), BF),
            pltpu.VMEM((2, 256, 256), BF),
            pltpu.VMEM((DIM, HID), BF),
            pltpu.VMEM((DIM, HID), BF),
            pltpu.VMEM((HID, DIM), BF),
            pltpu.VMEM((1152, HID), F32),
            pltpu.VMEM((1152, HID), F32),
            pltpu.VMEM((1152, HID), F32),
            pltpu.VMEM((1152, 128), F32),
            pltpu.VMEM((4, 16, 4, 16, QW), BF),
            pltpu.VMEM((4, 16, 16, HW), BF),
            pltpu.VMEM((4, 4, TOK, QW), BF),
            pltpu.VMEM((4, 4, TOK, QW), BF),
            pltpu.VMEM((16, 8, 128), F32),
            pltpu.VMEM((16, 8, 128), F32),
            pltpu.VMEM((8, 8, 128), F32),
            pltpu.VMEM((8, 8, 128), F32),
            DMA((3,)), DMA, DMA, DMA((2,)), DMA((2, 4, 4)), DMA((2,)), DMA((2, 4, 4)),
            DMA((3, 4)), DMA((3, 4)), DMA((3, 4)), DMA((3, 4)),
            DMA((3, 4)), DMA((3, 4)), DMA((4,)), DMA((4,)), DMA((4,)), DMA((4,)), DMA((4,)),
            DMA((4,)), DMA((4,)), DMA((4,)), DMA((4,)), DMA((2,)), DMA((2,)), DMA((3,)),
        ],
        compiler_params=pltpu.CompilerParams(
            collective_id=1, has_side_effects=True, vmem_limit_bytes=62 << 20
        ),
        cost_estimate=pl.CostEstimate(flops=30 << 30, bytes_accessed=30 << 20, transcendentals=1 << 20),
    )(tokens_x, grad_out, ids_t, probs_t, table, w_gate[0], w_up[0], w_down[0])
    grad_x, gpt, grad_gate, grad_up, grad_down = pl.pallas_call(
        hand_over,
        out_shape=(sds(TOK, DIM), sds(TOP, TOK), sds(DIM, HID), sds(DIM, HID), sds(HID, DIM)),
        in_specs=[ANY, VMEM, VMEM, ANY, ANY, ANY],
        out_specs=(ANY, VMEM, ANY, ANY, ANY),
        scratch_shapes=[
            pltpu.VMEM((TOK, DIM), BF),
            pltpu.VMEM((DIM, HID), BF),
            pltpu.VMEM((DIM, HID), BF),
            pltpu.VMEM((HID, DIM), BF),
            DMA((13,)), DMA((13,)),
        ],
        compiler_params=pltpu.CompilerParams(vmem_limit_bytes=60 << 20),
        cost_estimate=pl.CostEstimate(flops=1024, bytes_accessed=20 << 20, transcendentals=0),
    )(grad_x, gpt, probs_t, grad_gate, grad_up, grad_down)
    return grad_x, gpt.T, grad_gate[None], grad_up[None], grad_down[None]


def solution(mesh):
    token = P(("node", "local"), None)
    weight = P(("node", "local"), None, None)
    return jax.shard_map(
        shards,
        mesh=mesh,
        in_specs=(token, token, token, token, weight, weight, weight),
        out_specs=(token, token, weight, weight, weight),
        check_vma=False,
    )
```

```python
import functools

import jax
import jax.numpy as jnp
import numpy as np
from jax import lax
from jax.experimental import pallas as pl
from jax.experimental.pallas import tpu as pltpu
from jax.sharding import PartitionSpec as P

MESH = pl.DeviceIdType.MESH
BF = jnp.bfloat16
F32 = jnp.float32
TOK, DIM, HID, TOP = 128, 2048, 768, 8
QW = 512
HW = QW // 2
AXES_X = (0, 1, 2, 0)
AXES_DY = (1, 2, 0, 1)
AXES_PART = (2, 0, 1, 2)
OTHERS = {0: (1, 2), 1: (0, 2), 2: (0, 1)}


def unfold_table():
    table = np.zeros((3, 2, 128, 256), np.float32)
    for source in range(128):
        co = (source // 32, (source // 8) % 4, (source // 2) % 4)
        core = source % 2
        for axis in range(3):
            o1, o2 = OTHERS[axis]
            plane = co[o1] * 4 + co[o2]
            for half in range(2):
                table[axis, half, source, plane * 16 + half * 8 + co[axis] * 2 + core] = 1
    return table


class Place:
    def __init__(self):
        node, local = lax.axis_index("node"), lax.axis_index("local")
        self.pos = (lax.rem(node, 4), lax.div(node, 4), lax.div(local, 2))
        self.core = lax.rem(local, 2)
        self.mate_core = 1 - self.core

    def dev(self, co, core):
        return (co[1] * 4 + co[0], co[2] * 2 + core)

    def on_axis(self, axis, value, core):
        co = list(self.pos)
        co[axis] = value
        return self.dev(co, core)

    def on_plane(self, axis, first, second):
        co = list(self.pos)
        co[OTHERS[axis][0]], co[OTHERS[axis][1]] = first, second
        return self.dev(co, self.core)

    def plane(self, axis):
        o1, o2 = OTHERS[axis]
        return self.pos[o1] * 4 + self.pos[o2]

    def mate(self):
        return self.dev(self.pos, self.mate_core)

    def line(self, axis):
        idx = list(self.pos)
        idx[axis] = pl.ds(0, 4)
        return tuple(idx)


def plane_peer(place, axis, step):
    o1, o2 = OTHERS[axis]
    sign = 1 + 2 * place.core
    first = lax.rem(place.pos[o1] + sign * (lax.rem(step, 4) + lax.div(step, 4)), 4)
    second = lax.rem(place.pos[o2] + sign * lax.rem(step, 4), 4)
    return place.on_plane(axis, first, second), first * 4 + second


def remote(src, dst, send, recv, device):
    return pltpu.make_async_remote_copy(
        src_ref=src, dst_ref=dst, send_sem=send, recv_sem=recv, device_id=device, device_id_type=MESH
    )


def greet(place):
    barrier = pltpu.get_barrier_semaphore()

    def signal(device):
        pl.semaphore_signal(barrier, inc=1, device_id=device, device_id_type=MESH)

    count = 0
    for axis in range(3):
        for delta in range(1, 4):
            at = lax.rem(place.pos[axis] + delta, 4)
            signal(place.on_axis(axis, at, place.core))
            signal(place.on_axis(axis, at, place.mate_core))
            count += 2
        o1, o2 = OTHERS[axis]
        for d1 in range(1, 4):
            for d2 in range(1, 4):
                signal(place.on_plane(axis, lax.rem(place.pos[o1] + d1, 4), lax.rem(place.pos[o2] + d2, 4)))
                count += 1
    signal(place.mate())
    return count + 1


def await_greetings(count):
    pl.semaphore_wait(pltpu.get_barrier_semaphore(), count)


def build_select(rank_ref, weight_ref, axis, chip, main_ref, ninth_ref):
    row = lax.broadcasted_iota(jnp.int32, (16, 16, 128), 1)
    for core in range(2):
        at = axis * 8 + chip * 2 + core
        rank = jnp.broadcast_to(rank_ref[at][:, None, :], (16, 16, 128))
        if weight_ref is None:
            one = jnp.ones((16, 16, 128), F32)
        else:
            one = jnp.broadcast_to(weight_ref[at][:, None, :], (16, 16, 128))
        inside = (row < 8) if core == 0 else (row >= 8)
        lanes = pl.ds(core * 128, 128)
        main = jnp.where(inside & (rank == row - 8 * core), one, 0.0)
        main_ref[:, lanes] = main.reshape(256, 128).astype(BF)
        last = jnp.where(rank == 8, one, 0.0)
        for half in range(2):
            picked = jnp.where(row == half * 8 + chip * 2 + core, last, 0.0)
            ninth_ref[half, :, lanes] = picked.reshape(256, 128).astype(BF)


def dot(a, b, dims):
    return lax.dot_general(a, b, (dims, ((), ())), preferred_element_type=F32)


NN, NT, TN = ((1,), (0,)), ((1,), (1,)), ((0,), (0,))


def kernel(
    x_hbm, dy_hbm, ids_ref, probs_ref, table_ref, gate_hbm, up_hbm, down_hbm,
    gx_ref, gpt_ref, ggate_hbm, gup_hbm, gdown_hbm,
    xr_ref, x9_ref, dyr_ref, dy9_ref, h_ref, du_ref, dg_ref, info_ref, rank_ref, infos_ref, weight_ref,
    gath, send, send9, recv9, main_sel, ninth_sel, gate, up, down, g_acc, u_acc, dh_acc, row_sum,
    back, back9, mate_recv, line_recv, gp_ref, gp_recv, gp_part, gp_back,
    w_sem, info_send, info_recv, g1_send, g1_recv, g2_send, g2_recv, p_send, p_recv, p9_send, p9_recv,
    p_local, p9_local, c_send, c_recv, c_local, mc_send, mc_recv, m_send, m_recv, l_send, l_recv, gp_sems, gb_sems, out_sem,
):
    place = Place()
    pos, core = place.pos, place.core
    tokens = (x_hbm, dy_hbm)
    axes = (AXES_X, AXES_DY)
    landing = (xr_ref, dyr_ref)
    landing9 = (x9_ref, dy9_ref)
    for arr in range(2):
        for q in range(4):
            at = pos[axes[arr][q]]
            pltpu.make_async_copy(
                tokens[arr].at[:, pl.ds(q * QW, QW)], gath.at[arr, q, at, core], g1_recv.at[arr, q, at]
            ).start()
    loads = [
        pltpu.make_async_copy(src, dst, w_sem.at[i])
        for i, (src, dst) in enumerate(((gate_hbm, gate), (up_hbm, up), (down_hbm, down)))
    ]
    for load in loads:
        load.start()
    count = greet(place)
    info_ref[0:8, :] = ids_ref[...].astype(F32)
    info_ref[8:16, :] = probs_ref[...].astype(F32)
    for axis in range(3):
        infos_ref[axis * 8 + pos[axis] * 2 + core] = info_ref[...]
    await_greetings(count)

    for axis in range(3):
        mine = infos_ref.at[axis * 8 + pos[axis] * 2 + core]
        for delta in range(4):
            at = lax.rem(pos[axis] + delta, 4)
            if delta:
                remote(info_ref, mine, info_send, info_recv, place.on_axis(axis, at, core)).start()
            remote(info_ref, mine, info_send, info_recv, place.on_axis(axis, at, place.mate_core)).start()

    def gather(arr):
        for q in range(4):
            axis = axes[arr][q]
            for delta in (1, 3, 2):
                at = lax.rem(pos[axis] + delta, 4)
                remote(
                    tokens[arr].at[:, pl.ds(q * QW, QW)], gath.at[arr, q, pos[axis], core],
                    g1_send.at[arr], g1_recv.at[arr, q, pos[axis]], place.on_axis(axis, at, core),
                ).start()

    def forward(arr, q):
        axis = axes[arr][q]
        for delta in range(4):
            at = lax.rem(pos[axis] + delta, 4)
            block = gath.at[arr, q, at, core]
            pltpu.make_async_copy(block, block, g1_recv.at[arr, q, at]).wait()
            remote(block, block, g2_send.at[arr], g2_recv.at[arr, q, at], place.mate()).start()

    def select(arr, q):
        axis = axes[arr][q]
        for chip in range(4):
            build_select(rank_ref, weight_ref if arr else None, axis, chip, main_sel, ninth_sel)
            theirs = gath.at[arr, q, chip, place.mate_core]
            pltpu.make_async_copy(theirs, theirs, g2_recv.at[arr, q, chip]).wait()
            block = gath[arr, q, chip].reshape(256, QW)
            rows = dot(main_sel[...], block, NN)
            send[q, :, chip] = rows.reshape(16, 16, QW).astype(BF)
            last = dot(ninth_sel[0], block[:, :HW], NN) + dot(ninth_sel[1], block[:, HW:], NN)
            last = last.reshape(16, 16, HW).astype(BF)
            if chip:
                last = last + send9[q]
            send9[q] = last

    def scatter(arr, q, main=True):
        if arr < 2:
            axis = axes[arr][q]
            me = place.plane(axis)
            target = landing[arr].at[(*place.line(axis), pl.ds(0, 16), pl.ds(q * QW, QW))]
            target9 = recv9.at[arr, q, me]
        else:
            axis = AXES_PART[q]
            me = place.plane(axis)
            target = back.at[q, me]
            target9 = back9.at[q, me]
        sems = (p_send.at[arr, q], p_recv.at[arr, q])
        sems9 = (p9_send.at[arr, q], p9_recv.at[arr, q])

        def body(step, carry):
            device, index = plane_peer(place, axis, step)
            if main:
                remote(send.at[q, index], target, *sems, device).start()
            remote(send9.at[q, index], target9, *sems9, device).start()
            return carry

        lax.fori_loop(1, 16, body, 0)
        if main:
            pltpu.make_async_copy(send.at[q, me], target, p_local.at[arr, q]).start()
        pltpu.make_async_copy(send9.at[q, me], target9, p9_local.at[arr, q]).start()

    def sent(arr, q):
        whole = send.at[q, pl.ds(0, 15)]
        pltpu.make_async_copy(whole, whole, p_send.at[arr, q]).wait()
        whole = send9.at[q, pl.ds(0, 15)]
        pltpu.make_async_copy(whole, whole, p9_send.at[arr, q]).wait()

    def received9(arr, q):
        whole = send9.at[q, pl.ds(0, 15)]
        pltpu.make_async_copy(whole, whole, p9_recv.at[arr, q]).wait()
        one = send9.at[q, 0]
        pltpu.make_async_copy(one, one, p9_local.at[arr, q]).wait()

    def kept(arr, q):
        one = send.at[q, 0]
        pltpu.make_async_copy(one, one, p_local.at[arr, q]).wait()
        one = send9.at[q, 0]
        pltpu.make_async_copy(one, one, p9_local.at[arr, q]).wait()

    def received(arr, q):
        whole = send.at[q, pl.ds(0, 15)]
        pltpu.make_async_copy(whole, whole, p_recv.at[arr, q]).wait()
        whole = send9.at[q, pl.ds(0, 15)]
        pltpu.make_async_copy(whole, whole, p9_recv.at[arr, q]).wait()

    def unfold(arr, q):
        axis = axes[arr][q]
        folded = recv9[arr, q].reshape(256, HW)
        for half in range(2):
            rows = dot(table_ref[axis, half], folded, NN).astype(BF)
            landing9[arr][:, q * QW + half * HW:q * QW + (half + 1) * HW] = rows

    def arrive(arr, q):
        received(arr, q)
        if arr:
            kept(arr, q)
        unfold(arr, q)

    gather(0)
    gather(1)

    whole = infos_ref.at[pl.ds(0, 21)]
    pltpu.make_async_copy(whole, whole, info_recv).wait()
    before = (
        lax.broadcasted_iota(jnp.int32, (128, 128), 0) < lax.broadcasted_iota(jnp.int32, (128, 128), 1)
    ).astype(F32).astype(BF)
    index = lax.broadcasted_iota(jnp.int32, (16, 128), 0)
    for axis in range(3):
        co = list(pos)
        o1, o2 = OTHERS[axis]
        co[o1], co[o2] = lax.shift_right_logical(index, 2), lax.bitwise_and(index, 3)
        expert = ((co[1] * 4 + co[0]) * 8 + co[2] * 2 + core).astype(F32)
        for at in range(axis * 8, axis * 8 + 8):
            info = infos_ref[at]
            chosen = jnp.zeros((16, 128), F32)
            weight = jnp.zeros((16, 128), F32)
            for k in range(TOP):
                hit = info[k:k + 1, :] == expert
                chosen = chosen + jnp.where(hit, 1.0, 0.0)
                weight = weight + jnp.where(hit, jnp.broadcast_to(info[8 + k:9 + k, :], (16, 128)), 0.0)
            rank = dot(chosen.astype(BF), before, NN)
            rank_ref[at] = jnp.where(chosen > 0.0, rank, -1.0).astype(jnp.int32)
            weight_ref[at] = weight

    def accumulate(arr, q, outs):
        arrive(arr, q)

        def body(block, carry):
            lhs = landing[arr][block, :, :, :, q * QW:(q + 1) * QW].reshape(256, QW)
            for weights, dims, acc in outs:
                value = dot(lhs, weights, dims)
                if q:
                    value = value + acc[pl.ds(block * 256, 256), :]
                acc[pl.ds(block * 256, 256), :] = value
            return carry

        lax.fori_loop(0, 4, body, 0)
        lhs = landing9[arr][:, q * QW:(q + 1) * QW]
        for weights, dims, acc in outs:
            value = dot(lhs, weights, dims)
            if q:
                value = value + acc[1024:1152, :]
            acc[1024:1152, :] = value

    for q in range(4):
        forward(0, q)
        select(0, q)
        scatter(0, q)
    for load in loads:
        load.wait()
    for q in range(4):
        forward(1, q)
        sent(0, q)
        kept(0, q)
        select(1, q)
        scatter(1, q)
        rows = slice(q * QW, (q + 1) * QW)
        accumulate(0, q, ((gate[rows, :], NN, g_acc), (up[rows, :], NN, u_acc)))

    def activations(step, carry):
        rows = pl.ds(step * 32, 32)
        g, u = g_acc[rows, :], u_acc[rows, :]
        s = 0.5 * jnp.tanh(0.5 * g) + 0.5
        a = g * s
        h_ref[rows, :] = (a * u).astype(BF)
        g_acc[rows, :] = a
        u_acc[rows, :] = u * (s + a * (1.0 - s))
        return carry

    lax.fori_loop(0, 36, activations, 0)
    def down_grads(quarter):
        for tile in (quarter * 2, quarter * 2 + 1):
            cols = slice(tile * 256, (tile + 1) * 256)
            rhs = dyr_ref[:, :, :, :, cols].reshape(1024, 256)
            value = dot(h_ref[0:1024, :], rhs, TN) + dot(h_ref[1024:1152, :], dy9_ref[:, cols], TN)
            down[:, cols] = value.astype(BF)
            pltpu.make_async_copy(down.at[:, cols], gdown_hbm.at[:, cols], out_sem.at[2]).start()

    for q in range(3):
        accumulate(1, q, ((down[:, q * QW:(q + 1) * QW], NT, dh_acc),))
        down_grads(q)

    lane = lax.broadcasted_iota(jnp.int32, (32, 128), 1)
    slot = lax.bitwise_and(lax.broadcasted_iota(jnp.int32, (32, 128), 0), 7)

    def row_grads(step, carry):
        rows = pl.ds(step * 32, 32)
        dh = dh_acc[rows, :]
        du_ref[rows, :] = (dh * g_acc[rows, :]).astype(BF)
        dg_ref[rows, :] = (dh * u_acc[rows, :]).astype(BF)
        total = jnp.sum(dh * h_ref[rows, :].astype(F32), axis=1, keepdims=True)
        row_sum[rows, :] = jnp.where(lane == jnp.where(step < 32, slot, 8), total, 0.0)
        return carry

    def part_rows(rows, q):
        cols = slice(q * QW, (q + 1) * QW)
        value = dot(dg_ref[rows, :], gate[cols, :], NT) + dot(du_ref[rows, :], up[cols, :], NT)
        return value.astype(BF)

    def part_ninth(q):
        axis = AXES_PART[q]
        value = part_rows(slice(1024, 1152), q)
        folded = dot(table_ref[axis, 0], value[:, :HW], TN) + dot(table_ref[axis, 1], value[:, HW:], TN)
        send9[q] = folded.astype(BF).reshape(16, 16, HW)

    def part_block(q, block):
        axis = AXES_PART[q]
        value = part_rows(pl.ds(pl.multiple_of(block * 256, 256), 256), q).reshape(4, 4, 16, QW)
        if axis == 0:
            send[q, :, block] = value.reshape(16, 16, QW)
        elif axis == 1:
            for chip in range(4):
                send[q, pl.ds(block * 4, 4), chip] = value[chip]
        else:
            send[q, pl.ds(block * 4, 4)] = value

    last = slice(3 * QW, 4 * QW)
    sent(1, 0)
    received(1, 3)
    kept(1, 3)
    me_z = place.plane(2)

    def first_back(step, carry):
        block = lax.rem(pos[0] + step, 4)
        rows = pl.ds(pl.multiple_of(block * 256, 256), 256)
        lhs = dyr_ref[block, :, :, :, last].reshape(256, QW)
        dh_acc[rows, :] = dh_acc[rows, :] + dot(lhs, down[:, last], NT)

        def block_grads(i, carry):
            return row_grads(block * 8 + i, carry)

        lax.fori_loop(0, 8, block_grads, 0, unroll=2)
        part_block(0, block)
        for turn in range(4):
            second = lax.rem(pos[1] + turn, 4)
            index = block * 4 + second
            device = place.on_plane(2, block, second)

            def away():
                remote(send.at[0, index], back.at[0, me_z], p_send.at[2, 0], p_recv.at[2, 0], device).start()

            if turn == 0:
                @pl.when(step == 0)
                def _():
                    pltpu.make_async_copy(send.at[0, index], back.at[0, me_z], p_local.at[2, 0]).start()

                pl.when(step > 0)(away)
            else:
                away()
        return carry

    lax.fori_loop(0, 4, first_back, 0)
    unfold(1, 3)
    dh_acc[1024:1152, :] = dh_acc[1024:1152, :] + dot(dy9_ref[:, last], down[:, last], NT)
    lax.fori_loop(32, 36, row_grads, 0)
    part_ninth(0)
    scatter(2, 0, main=False)
    sums = jnp.sum(row_sum[0:1024, :].reshape(128, 8, 128), axis=1) + row_sum[1024:1152, :]
    gp_ref[...] = sums.reshape(16, 8, 128)

    def send_gp(step, carry):
        device, index = plane_peer(place, 2, step)
        remote(gp_ref.at[index], gp_recv.at[me_z], gp_sems.at[0], gp_sems.at[1], device).start()
        return carry

    lax.fori_loop(1, 16, send_gp, 0)
    pltpu.make_async_copy(gp_ref.at[me_z], gp_recv.at[me_z], gp_sems.at[1]).start()

    def part_body(q):
        def body(block, carry):
            part_block(q, block)
            return carry

        return body

    for q in range(1, 4):
        sent(1, q)
        part_ninth(q)
        lax.fori_loop(0, 4, part_body(q), 0)
        scatter(2, q, main=q < 3)

    line_chips = [lax.rem(pos[AXES_PART[3]] + delta, 4) for delta in (2, 1, 3, 0)]
    me_last = place.plane(AXES_PART[3])
    for turn, chip in enumerate(line_chips):
        def chip_away(step, carry):
            device, index = plane_peer(place, AXES_PART[3], step)
            remote(
                send.at[3, index, chip], back.at[3, me_last, chip], c_send.at[turn], c_recv.at[turn], device
            ).start()
            return carry

        lax.fori_loop(1, 16, chip_away, 0)
        pltpu.make_async_copy(send.at[3, me_last, chip], back.at[3, me_last, chip], c_local.at[turn]).start()

    whole = gath.at[0, :, :, 0]
    pltpu.make_async_copy(whole, whole, g2_send.at[0]).wait()

    def weight_grads(quarter):
        for tile in (quarter * 2, quarter * 2 + 1):
            cols = slice(tile * 256, (tile + 1) * 256)
            lhs = xr_ref[:, :, :, :, cols].reshape(1024, 256)
            lhs9 = x9_ref[:, cols]
            for which, (rows_ref, buffer, out) in enumerate(((dg_ref, gate, ggate_hbm), (du_ref, up, gup_hbm))):
                value = dot(lhs, rows_ref[0:1024, :], TN) + dot(lhs9, rows_ref[1024:1152, :], TN)
                buffer[cols, :] = value.astype(BF)
                pltpu.make_async_copy(buffer.at[cols], out.at[cols], out_sem.at[which]).start()

    def own(q, chip):
        return pl.ds(pl.multiple_of(((q % 2) * 4 + chip) * 128, 128), 128)

    def combine_chip(q, chip, ready=None):
        build_select(rank_ref, None, AXES_PART[q], chip, main_sel, ninth_sel)
        if ready is not None:
            ready()
        last = back9[q].reshape(256, HW)
        value = dot(main_sel[...], back[q, :, chip].reshape(256, QW), TN)
        value = value + jnp.concatenate([dot(ninth_sel[0], last, TN), dot(ninth_sel[1], last, TN)], axis=1)
        mine = core == 0
        g_acc[own(q, chip), :QW] = jnp.where(mine, value[:128], value[128:])
        gath[0, q, chip, 0] = jnp.where(mine, value[128:], value[:128]).astype(BF)

    def combine(q):
        received(2, q)
        kept(2, q)
        for chip in range(4):
            combine_chip(q, chip)
        remote(gath.at[0, q, :, 0], mate_recv.at[q], m_send.at[q], m_recv.at[q], place.mate()).start()

    def to_line(q):
        axis = AXES_PART[q]
        whole = mate_recv.at[q]
        pltpu.make_async_copy(whole, whole, m_recv.at[q]).wait()
        for chip in range(4):
            gath[0, q, chip, 1] = (g_acc[own(q, chip), :QW] + mate_recv[q, chip].astype(F32)).astype(BF)
        for delta in (1, 3, 2):
            at = lax.rem(pos[axis] + delta, 4)
            remote(
                gath.at[0, q, at, 1], line_recv.at[q, pos[axis]], l_send.at[q], l_recv.at[q],
                place.on_axis(axis, at, core),
            ).start()
        pltpu.make_async_copy(gath.at[0, q, pos[axis], 1], line_recv.at[q, pos[axis]], l_recv.at[q]).start()

    def combine_last(turn):
        chip = line_chips[turn]

        def ready():
            whole = send.at[3, pl.ds(0, 15), 0]
            pltpu.make_async_copy(whole, whole, c_recv.at[turn]).wait()
            one = send.at[3, 0, 0]
            pltpu.make_async_copy(one, one, c_local.at[turn]).wait()

        combine_chip(3, chip, ready)
        remote(
            gath.at[0, 3, chip, 0], mate_recv.at[3, chip], mc_send.at[turn], mc_recv.at[turn], place.mate()
        ).start()

    def line_last(turn):
        chip = line_chips[turn]
        one = mate_recv.at[3, chip]
        pltpu.make_async_copy(one, one, mc_recv.at[turn]).wait()
        gath[0, 3, chip, 1] = (g_acc[own(3, chip), :QW] + mate_recv[3, chip].astype(F32)).astype(BF)
        here = line_recv.at[3, pos[AXES_PART[3]]]
        if turn < 3:
            device = place.on_axis(AXES_PART[3], chip, core)
            remote(gath.at[0, 3, chip, 1], here, l_send.at[3], l_recv.at[3], device).start()
        else:
            pltpu.make_async_copy(gath.at[0, 3, chip, 1], here, l_recv.at[3]).start()

    def finish(q):
        whole = line_recv.at[q]
        pltpu.make_async_copy(whole, whole, l_recv.at[q]).wait()
        total = line_recv[q, 0].astype(F32) + line_recv[q, 1].astype(F32)
        total = total + line_recv[q, 2].astype(F32) + line_recv[q, 3].astype(F32)
        gx_ref[:, q * QW:(q + 1) * QW] = total.astype(BF)

    def probs_back():
        pltpu.make_async_copy(gp_recv, gp_recv, gp_sems.at[1]).wait()
        expert = ((index_y * 4 + index_x) * 8 + pos[2] * 2 + core).astype(F32)
        for source in range(8):
            rank = rank_ref[16 + source]
            values = gp_recv[:, source, :]
            info = infos_ref[16 + source]
            spread = jnp.zeros((16, 128), F32)
            for j in range(9):
                spread = jnp.where(rank == j, values[:, j:j + 1], spread)
            for k in range(TOP):
                hit = info[k:k + 1, :] == expert
                gp_part[source, k:k + 1, :] = jnp.sum(jnp.where(hit, spread, 0.0), axis=0, keepdims=True)
        mine = pos[2] * 2 + core
        for delta in range(4):
            at = lax.rem(pos[2] + delta, 4)
            for whose in ((core, place.mate_core) if delta else (place.mate_core,)):
                remote(
                    gp_part.at[at * 2 + whose], gp_back.at[mine], gb_sems.at[0], gb_sems.at[1],
                    place.on_axis(2, at, whose),
                ).start()
        pltpu.make_async_copy(gp_part.at[mine], gp_back.at[mine], gb_sems.at[1]).start()

    index_x, index_y = lax.shift_right_logical(index, 2), lax.bitwise_and(index, 3)
    weight_grads(0)
    probs_back()
    combine(0)
    weight_grads(1)
    to_line(0)
    combine(1)
    weight_grads(2)
    to_line(1)
    combine(2)
    finish(0)
    to_line(2)
    received9(2, 3)
    combine_last(0)
    combine_last(1)
    line_last(0)
    combine_last(2)
    line_last(1)
    combine_last(3)
    line_last(2)
    line_last(3)
    finish(1)
    down_grads(3)
    weight_grads(3)
    pltpu.make_async_copy(gp_back, gp_back, gb_sems.at[1]).wait()
    total = gp_back[0]
    for i in range(1, 8):
        total = total + gp_back[i]
    gpt_ref[...] = total
    finish(2)

    for which, (buffer, out) in enumerate(((gate, ggate_hbm), (up, gup_hbm), (down, gdown_hbm))):
        pltpu.make_async_copy(buffer, out, out_sem.at[which]).wait()
    whole = infos_ref.at[pl.ds(0, 21)]
    pltpu.make_async_copy(whole, whole, info_send).wait()
    for arr in range(2):
        whole = gath.at[arr, :, pl.ds(0, 3), 0]
        pltpu.make_async_copy(whole, whole, g1_send.at[arr]).wait()
    whole = gath.at[1, :, :, 0]
    pltpu.make_async_copy(whole, whole, g2_send.at[1]).wait()
    whole = gp_recv.at[pl.ds(0, 15)]
    pltpu.make_async_copy(whole, whole, gp_sems.at[0]).wait()
    whole = gp_back.at[pl.ds(0, 7)]
    pltpu.make_async_copy(whole, whole, gb_sems.at[0]).wait()
    for q in range(3):
        sent(2, q)
        whole = mate_recv.at[q]
        pltpu.make_async_copy(whole, whole, m_send.at[q]).wait()
    whole = send9.at[3, pl.ds(0, 15)]
    pltpu.make_async_copy(whole, whole, p9_send.at[2, 3]).wait()
    for turn in range(4):
        whole = send.at[3, pl.ds(0, 15), 0]
        pltpu.make_async_copy(whole, whole, c_send.at[turn]).wait()
        one = mate_recv.at[3, 0]
        pltpu.make_async_copy(one, one, mc_send.at[turn]).wait()
    for q in range(4):
        whole = line_recv.at[q, pl.ds(0, 3)]
        pltpu.make_async_copy(whole, whole, l_send.at[q]).wait()
    finish(3)


def hand_over(
    gx_ref, gpt_ref, probs_ref, gate_ref, up_ref, down_ref, gx_out, probs_out, gate_out, up_out, down_out,
    gx, gate, up, down, in_sems, out_sems,
):
    steps = []
    for src, via, dst in (
        (gate_ref, gate, gate_out), (up_ref, up, up_out), (down_ref, down, down_out), (gx_ref, gx, gx_out)
    ):
        rows = max(src.shape[0] // 4, 128)
        for start in range(0, src.shape[0], rows):
            part, n = pl.ds(start, rows), len(steps)
            steps.append((
                pltpu.make_async_copy(src.at[part], via.at[part], in_sems.at[n]),
                pltpu.make_async_copy(via.at[part], dst.at[part], out_sems.at[n]),
            ))
    for load, _ in steps:
        load.start()
    probs_out[...] = (gpt_ref[...] / probs_ref[...].astype(F32)).astype(BF)
    for load, store in steps:
        load.wait()
        store.start()
    for _, store in steps:
        store.wait()


VMEM = pl.BlockSpec(memory_space=pltpu.VMEM)
ANY = pl.BlockSpec(memory_space=pl.ANY)
DMA = pltpu.SemaphoreType.DMA


def sds(*shape, dtype=BF):
    return jax.ShapeDtypeStruct(shape, dtype)


def shards(tokens_x, grad_out, expert_ids, probs, w_gate, w_up, w_down):
    ids_t, probs_t = expert_ids.T, probs.T
    table = jnp.asarray(unfold_table(), BF)
    grad_x, gpt, grad_gate, grad_up, grad_down = pl.pallas_call(
        kernel,
        out_shape=(
            sds(TOK, DIM), sds(TOP, TOK, dtype=F32), sds(DIM, HID), sds(DIM, HID), sds(HID, DIM),
        ),
        in_specs=[ANY, ANY, VMEM, VMEM, VMEM, ANY, ANY, ANY],
        out_specs=(VMEM, VMEM, ANY, ANY, ANY),
        scratch_shapes=[
            pltpu.VMEM((4, 4, 4, 16, DIM), BF),
            pltpu.VMEM((128, DIM), BF),
            pltpu.VMEM((4, 4, 4, 16, DIM), BF),
            pltpu.VMEM((128, DIM), BF),
            pltpu.VMEM((1152, HID), BF),
            pltpu.VMEM((1152, HID), BF),
            pltpu.VMEM((1152, HID), BF),
            pltpu.VMEM((16, 128), F32),
            pltpu.VMEM((24, 16, 128), jnp.int32),
            pltpu.VMEM((24, 16, 128), F32),
            pltpu.VMEM((24, 16, 128), F32),
            pltpu.VMEM((2, 4, 4, 2, TOK, QW), BF),
            pltpu.VMEM((4, 16, 4, 16, QW), BF),
            pltpu.VMEM((4, 16, 16, HW), BF),
            pltpu.VMEM((2, 4, 16, 16, HW), BF),
            pltpu.VMEM((256, 256), BF),
            pltpu.VMEM((2, 256, 256), BF),
            pltpu.VMEM((DIM, HID), BF),
            pltpu.VMEM((DIM, HID), BF),
            pltpu.VMEM((HID, DIM), BF),
            pltpu.VMEM((1152, HID), F32),
            pltpu.VMEM((1152, HID), F32),
            pltpu.VMEM((1152, HID), F32),
            pltpu.VMEM((1152, 128), F32),
            pltpu.VMEM((4, 16, 4, 16, QW), BF),
            pltpu.VMEM((4, 16, 16, HW), BF),
            pltpu.VMEM((4, 4, TOK, QW), BF),
            pltpu.VMEM((4, 4, TOK, QW), BF),
            pltpu.VMEM((16, 8, 128), F32),
            pltpu.VMEM((16, 8, 128), F32),
            pltpu.VMEM((8, 8, 128), F32),
            pltpu.VMEM((8, 8, 128), F32),
            DMA((3,)), DMA, DMA, DMA((2,)), DMA((2, 4, 4)), DMA((2,)), DMA((2, 4, 4)),
            DMA((3, 4)), DMA((3, 4)), DMA((3, 4)), DMA((3, 4)),
            DMA((3, 4)), DMA((3, 4)), DMA((4,)), DMA((4,)), DMA((4,)), DMA((4,)), DMA((4,)),
            DMA((4,)), DMA((4,)), DMA((4,)), DMA((4,)), DMA((2,)), DMA((2,)), DMA((3,)),
        ],
        compiler_params=pltpu.CompilerParams(
            collective_id=1, has_side_effects=True, vmem_limit_bytes=62 << 20
        ),
        cost_estimate=pl.CostEstimate(flops=30 << 30, bytes_accessed=30 << 20, transcendentals=1 << 20),
    )(tokens_x, grad_out, ids_t, probs_t, table, w_gate[0], w_up[0], w_down[0])
    grad_x, gpt, grad_gate, grad_up, grad_down = pl.pallas_call(
        hand_over,
        out_shape=(sds(TOK, DIM), sds(TOP, TOK), sds(DIM, HID), sds(DIM, HID), sds(HID, DIM)),
        in_specs=[ANY, VMEM, VMEM, ANY, ANY, ANY],
        out_specs=(ANY, VMEM, ANY, ANY, ANY),
        scratch_shapes=[
            pltpu.VMEM((TOK, DIM), BF),
            pltpu.VMEM((DIM, HID), BF),
            pltpu.VMEM((DIM, HID), BF),
            pltpu.VMEM((HID, DIM), BF),
            DMA((13,)), DMA((13,)),
        ],
        compiler_params=pltpu.CompilerParams(vmem_limit_bytes=60 << 20),
        cost_estimate=pl.CostEstimate(flops=1024, bytes_accessed=20 << 20, transcendentals=0),
    )(grad_x, gpt, probs_t, grad_gate, grad_up, grad_down)
    return grad_x, gpt.T, grad_gate[None], grad_up[None], grad_down[None]


def solution(mesh):
    token = P(("node", "local"), None)
    weight = P(("node", "local"), None, None)
    return jax.shard_map(
        shards,
        mesh=mesh,
        in_specs=(token, token, token, token, weight, weight, weight),
        out_specs=(token, token, weight, weight, weight),
        check_vma=False,
    )
```

```python
import functools

import jax
import jax.numpy as jnp
import numpy as np
from jax import lax
from jax.experimental import pallas as pl
from jax.experimental.pallas import tpu as pltpu
from jax.sharding import PartitionSpec as P

MESH = pl.DeviceIdType.MESH
BF = jnp.bfloat16
F32 = jnp.float32
TOK, DIM, HID, TOP = 128, 2048, 768, 8
QW = 512
HW = QW // 2
AXES_X = (0, 1, 2, 0)
AXES_DY = (1, 2, 0, 1)
AXES_PART = (2, 0, 1, 2)
OTHERS = {0: (1, 2), 1: (0, 2), 2: (0, 1)}


def unfold_table():
    table = np.zeros((3, 2, 128, 256), np.float32)
    for source in range(128):
        co = (source // 32, (source // 8) % 4, (source // 2) % 4)
        core = source % 2
        for axis in range(3):
            o1, o2 = OTHERS[axis]
            plane = co[o1] * 4 + co[o2]
            for half in range(2):
                table[axis, half, source, plane * 16 + half * 8 + co[axis] * 2 + core] = 1
    return table


class Place:
    def __init__(self):
        node, local = lax.axis_index("node"), lax.axis_index("local")
        self.pos = (lax.rem(node, 4), lax.div(node, 4), lax.div(local, 2))
        self.core = lax.rem(local, 2)
        self.mate_core = 1 - self.core

    def dev(self, co, core):
        return (co[1] * 4 + co[0], co[2] * 2 + core)

    def on_axis(self, axis, value, core):
        co = list(self.pos)
        co[axis] = value
        return self.dev(co, core)

    def on_plane(self, axis, first, second):
        co = list(self.pos)
        co[OTHERS[axis][0]], co[OTHERS[axis][1]] = first, second
        return self.dev(co, self.core)

    def plane(self, axis):
        o1, o2 = OTHERS[axis]
        return self.pos[o1] * 4 + self.pos[o2]

    def mate(self):
        return self.dev(self.pos, self.mate_core)

    def line(self, axis):
        idx = list(self.pos)
        idx[axis] = pl.ds(0, 4)
        return tuple(idx)


def plane_peer(place, axis, step):
    o1, o2 = OTHERS[axis]
    sign = 1 + 2 * place.core
    first = lax.rem(place.pos[o1] + sign * (lax.rem(step, 4) + lax.div(step, 4)), 4)
    second = lax.rem(place.pos[o2] + sign * lax.rem(step, 4), 4)
    return place.on_plane(axis, first, second), first * 4 + second


def remote(src, dst, send, recv, device):
    return pltpu.make_async_remote_copy(
        src_ref=src, dst_ref=dst, send_sem=send, recv_sem=recv, device_id=device, device_id_type=MESH
    )


def greet(place):
    barrier = pltpu.get_barrier_semaphore()

    def signal(device):
        pl.semaphore_signal(barrier, inc=1, device_id=device, device_id_type=MESH)

    count = 0
    for axis in range(3):
        for delta in range(1, 4):
            at = lax.rem(place.pos[axis] + delta, 4)
            signal(place.on_axis(axis, at, place.core))
            signal(place.on_axis(axis, at, place.mate_core))
            count += 2
        o1, o2 = OTHERS[axis]
        for d1 in range(1, 4):
            for d2 in range(1, 4):
                signal(place.on_plane(axis, lax.rem(place.pos[o1] + d1, 4), lax.rem(place.pos[o2] + d2, 4)))
                count += 1
    signal(place.mate())
    return count + 1


def await_greetings(count):
    pl.semaphore_wait(pltpu.get_barrier_semaphore(), count)


def build_select(rank_ref, weight_ref, axis, chip, main_ref, ninth_ref):
    row = lax.broadcasted_iota(jnp.int32, (16, 16, 128), 1)
    for core in range(2):
        at = axis * 8 + chip * 2 + core
        rank = jnp.broadcast_to(rank_ref[at][:, None, :], (16, 16, 128))
        if weight_ref is None:
            one = jnp.ones((16, 16, 128), F32)
        else:
            one = jnp.broadcast_to(weight_ref[at][:, None, :], (16, 16, 128))
        inside = (row < 8) if core == 0 else (row >= 8)
        lanes = pl.ds(core * 128, 128)
        main = jnp.where(inside & (rank == row - 8 * core), one, 0.0)
        main_ref[:, lanes] = main.reshape(256, 128).astype(BF)
        last = jnp.where(rank == 8, one, 0.0)
        for half in range(2):
            picked = jnp.where(row == half * 8 + chip * 2 + core, last, 0.0)
            ninth_ref[half, :, lanes] = picked.reshape(256, 128).astype(BF)


def dot(a, b, dims):
    return lax.dot_general(a, b, (dims, ((), ())), preferred_element_type=F32)


NN, NT, TN = ((1,), (0,)), ((1,), (1,)), ((0,), (0,))


def kernel(
    x_hbm, dy_hbm, ids_ref, probs_ref, table_ref, gate_hbm, up_hbm, down_hbm,
    gx_ref, gpt_ref, ggate_hbm, gup_hbm, gdown_hbm,
    xr_ref, x9_ref, dyr_ref, dy9_ref, h_ref, du_ref, dg_ref, info_ref, rank_ref, infos_ref, weight_ref,
    gath, send, send9, recv9, main_sel, ninth_sel, gate, up, down, g_acc, u_acc, dh_acc, row_sum,
    back, back9, mate_recv, line_recv, gp_ref, gp_recv, gp_part, gp_back,
    w_sem, info_send, info_recv, g1_send, g1_recv, g2_send, g2_recv, p_send, p_recv, p9_send, p9_recv,
    p_local, p9_local, c_send, c_recv, c_local, mc_send, mc_recv, m_send, m_recv, l_send, l_recv, gp_sems, gb_sems, out_sem,
):
    place = Place()
    pos, core = place.pos, place.core
    tokens = (x_hbm, dy_hbm)
    axes = (AXES_X, AXES_DY)
    landing = (xr_ref, dyr_ref)
    landing9 = (x9_ref, dy9_ref)
    for arr in range(2):
        for q in range(4):
            at = pos[axes[arr][q]]
            pltpu.make_async_copy(
                tokens[arr].at[:, pl.ds(q * QW, QW)], gath.at[arr, q, at, core], g1_recv.at[arr, q, at]
            ).start()
    loads = [
        pltpu.make_async_copy(src, dst, w_sem.at[i])
        for i, (src, dst) in enumerate(((gate_hbm, gate), (up_hbm, up), (down_hbm, down)))
    ]
    for load in loads:
        load.start()
    count = greet(place)
    info_ref[0:8, :] = ids_ref[...].astype(F32)
    info_ref[8:16, :] = probs_ref[...].astype(F32)
    for axis in range(3):
        infos_ref[axis * 8 + pos[axis] * 2 + core] = info_ref[...]
    await_greetings(count)

    for axis in range(3):
        mine = infos_ref.at[axis * 8 + pos[axis] * 2 + core]
        for delta in range(4):
            at = lax.rem(pos[axis] + delta, 4)
            if delta:
                remote(info_ref, mine, info_send, info_recv, place.on_axis(axis, at, core)).start()
            remote(info_ref, mine, info_send, info_recv, place.on_axis(axis, at, place.mate_core)).start()

    def gather(arr):
        for q in range(4):
            axis = axes[arr][q]
            for delta in (1, 3, 2):
                at = lax.rem(pos[axis] + delta, 4)
                remote(
                    tokens[arr].at[:, pl.ds(q * QW, QW)], gath.at[arr, q, pos[axis], core],
                    g1_send.at[arr], g1_recv.at[arr, q, pos[axis]], place.on_axis(axis, at, core),
                ).start()

    def forward(arr, q):
        axis = axes[arr][q]
        for delta in range(4):
            at = lax.rem(pos[axis] + delta, 4)
            block = gath.at[arr, q, at, core]
            pltpu.make_async_copy(block, block, g1_recv.at[arr, q, at]).wait()
            remote(block, block, g2_send.at[arr], g2_recv.at[arr, q, at], place.mate()).start()

    def select(arr, q):
        axis = axes[arr][q]
        for chip in range(4):
            build_select(rank_ref, weight_ref if arr else None, axis, chip, main_sel, ninth_sel)
            theirs = gath.at[arr, q, chip, place.mate_core]
            pltpu.make_async_copy(theirs, theirs, g2_recv.at[arr, q, chip]).wait()
            block = gath[arr, q, chip].reshape(256, QW)
            rows = dot(main_sel[...], block, NN)
            send[q, :, chip] = rows.reshape(16, 16, QW).astype(BF)
            last = dot(ninth_sel[0], block[:, :HW], NN) + dot(ninth_sel[1], block[:, HW:], NN)
            last = last.reshape(16, 16, HW).astype(BF)
            if chip:
                last = last + send9[q]
            send9[q] = last

    def scatter(arr, q, main=True):
        if arr < 2:
            axis = axes[arr][q]
            me = place.plane(axis)
            target = landing[arr].at[(*place.line(axis), pl.ds(0, 16), pl.ds(q * QW, QW))]
            target9 = recv9.at[arr, q, me]
        else:
            axis = AXES_PART[q]
            me = place.plane(axis)
            target = back.at[q, me]
            target9 = back9.at[q, me]
        sems = (p_send.at[arr, q], p_recv.at[arr, q])
        sems9 = (p9_send.at[arr, q], p9_recv.at[arr, q])

        def body(step, carry):
            device, index = plane_peer(place, axis, step)
            if main:
                remote(send.at[q, index], target, *sems, device).start()
            remote(send9.at[q, index], target9, *sems9, device).start()
            return carry

        lax.fori_loop(1, 16, body, 0)
        if main:
            pltpu.make_async_copy(send.at[q, me], target, p_local.at[arr, q]).start()
        pltpu.make_async_copy(send9.at[q, me], target9, p9_local.at[arr, q]).start()

    def sent(arr, q):
        whole = send.at[q, pl.ds(0, 15)]
        pltpu.make_async_copy(whole, whole, p_send.at[arr, q]).wait()
        whole = send9.at[q, pl.ds(0, 15)]
        pltpu.make_async_copy(whole, whole, p9_send.at[arr, q]).wait()

    def received9(arr, q):
        whole = send9.at[q, pl.ds(0, 15)]
        pltpu.make_async_copy(whole, whole, p9_recv.at[arr, q]).wait()
        one = send9.at[q, 0]
        pltpu.make_async_copy(one, one, p9_local.at[arr, q]).wait()

    def kept(arr, q):
        one = send.at[q, 0]
        pltpu.make_async_copy(one, one, p_local.at[arr, q]).wait()
        one = send9.at[q, 0]
        pltpu.make_async_copy(one, one, p9_local.at[arr, q]).wait()

    def received(arr, q):
        whole = send.at[q, pl.ds(0, 15)]
        pltpu.make_async_copy(whole, whole, p_recv.at[arr, q]).wait()
        whole = send9.at[q, pl.ds(0, 15)]
        pltpu.make_async_copy(whole, whole, p9_recv.at[arr, q]).wait()

    def unfold(arr, q):
        axis = axes[arr][q]
        folded = recv9[arr, q].reshape(256, HW)
        for half in range(2):
            rows = dot(table_ref[axis, half], folded, NN).astype(BF)
            landing9[arr][:, q * QW + half * HW:q * QW + (half + 1) * HW] = rows

    def arrive(arr, q):
        received(arr, q)
        if arr:
            kept(arr, q)
        unfold(arr, q)

    gather(0)
    gather(1)

    whole = infos_ref.at[pl.ds(0, 21)]
    pltpu.make_async_copy(whole, whole, info_recv).wait()
    before = (
        lax.broadcasted_iota(jnp.int32, (128, 128), 0) < lax.broadcasted_iota(jnp.int32, (128, 128), 1)
    ).astype(F32).astype(BF)
    index = lax.broadcasted_iota(jnp.int32, (16, 128), 0)
    for axis in range(3):
        co = list(pos)
        o1, o2 = OTHERS[axis]
        co[o1], co[o2] = lax.shift_right_logical(index, 2), lax.bitwise_and(index, 3)
        expert = ((co[1] * 4 + co[0]) * 8 + co[2] * 2 + core).astype(F32)
        for at in range(axis * 8, axis * 8 + 8):
            info = infos_ref[at]
            chosen = jnp.zeros((16, 128), F32)
            weight = jnp.zeros((16, 128), F32)
            for k in range(TOP):
                hit = info[k:k + 1, :] == expert
                chosen = chosen + jnp.where(hit, 1.0, 0.0)
                weight = weight + jnp.where(hit, jnp.broadcast_to(info[8 + k:9 + k, :], (16, 128)), 0.0)
            rank = dot(chosen.astype(BF), before, NN)
            rank_ref[at] = jnp.where(chosen > 0.0, rank, -1.0).astype(jnp.int32)
            weight_ref[at] = weight

    def accumulate(arr, q, outs):
        arrive(arr, q)

        def body(block, carry):
            lhs = landing[arr][block, :, :, :, q * QW:(q + 1) * QW].reshape(256, QW)
            for weights, dims, acc in outs:
                value = dot(lhs, weights, dims)
                if q:
                    value = value + acc[pl.ds(block * 256, 256), :]
                acc[pl.ds(block * 256, 256), :] = value
            return carry

        lax.fori_loop(0, 4, body, 0)
        lhs = landing9[arr][:, q * QW:(q + 1) * QW]
        for weights, dims, acc in outs:
            value = dot(lhs, weights, dims)
            if q:
                value = value + acc[1024:1152, :]
            acc[1024:1152, :] = value

    for q in range(4):
        forward(0, q)
        select(0, q)
        scatter(0, q)
    for load in loads:
        load.wait()
    for q in range(4):
        forward(1, q)
        sent(0, q)
        kept(0, q)
        select(1, q)
        scatter(1, q)
        rows = slice(q * QW, (q + 1) * QW)
        accumulate(0, q, ((gate[rows, :], NN, g_acc), (up[rows, :], NN, u_acc)))

    def activations(step, carry):
        rows = pl.ds(step * 32, 32)
        g, u = g_acc[rows, :], u_acc[rows, :]
        s = 0.5 * jnp.tanh(0.5 * g) + 0.5
        a = g * s
        h_ref[rows, :] = (a * u).astype(BF)
        g_acc[rows, :] = a
        u_acc[rows, :] = u * (s + a * (1.0 - s))
        return carry

    lax.fori_loop(0, 36, activations, 0)
    def down_grads(quarter):
        for tile in (quarter * 2, quarter * 2 + 1):
            cols = slice(tile * 256, (tile + 1) * 256)
            rhs = dyr_ref[:, :, :, :, cols].reshape(1024, 256)
            value = dot(h_ref[0:1024, :], rhs, TN) + dot(h_ref[1024:1152, :], dy9_ref[:, cols], TN)
            down[:, cols] = value.astype(BF)
            pltpu.make_async_copy(down.at[:, cols], gdown_hbm.at[:, cols], out_sem.at[2]).start()

    for q in range(3):
        accumulate(1, q, ((down[:, q * QW:(q + 1) * QW], NT, dh_acc),))
        down_grads(q)

    lane = lax.broadcasted_iota(jnp.int32, (32, 128), 1)
    slot = lax.bitwise_and(lax.broadcasted_iota(jnp.int32, (32, 128), 0), 7)

    def row_grads(step, carry):
        rows = pl.ds(step * 32, 32)
        dh = dh_acc[rows, :]
        du_ref[rows, :] = (dh * g_acc[rows, :]).astype(BF)
        dg_ref[rows, :] = (dh * u_acc[rows, :]).astype(BF)
        total = jnp.sum(dh * h_ref[rows, :].astype(F32), axis=1, keepdims=True)
        row_sum[rows, :] = jnp.where(lane == jnp.where(step < 32, slot, 8), total, 0.0)
        return carry

    def part_rows(rows, q):
        cols = slice(q * QW, (q + 1) * QW)
        value = dot(dg_ref[rows, :], gate[cols, :], NT) + dot(du_ref[rows, :], up[cols, :], NT)
        return value.astype(BF)

    def part_ninth(q):
        axis = AXES_PART[q]
        value = part_rows(slice(1024, 1152), q)
        folded = dot(table_ref[axis, 0], value[:, :HW], TN) + dot(table_ref[axis, 1], value[:, HW:], TN)
        send9[q] = folded.astype(BF).reshape(16, 16, HW)

    def part_block(q, block):
        axis = AXES_PART[q]
        value = part_rows(pl.ds(pl.multiple_of(block * 256, 256), 256), q).reshape(4, 4, 16, QW)
        if axis == 0:
            send[q, :, block] = value.reshape(16, 16, QW)
        elif axis == 1:
            for chip in range(4):
                send[q, pl.ds(block * 4, 4), chip] = value[chip]
        else:
            send[q, pl.ds(block * 4, 4)] = value

    last = slice(3 * QW, 4 * QW)
    sent(1, 0)
    received(1, 3)
    kept(1, 3)
    me_z = place.plane(2)

    def first_back(step, carry):
        block = lax.rem(pos[0] + step, 4)
        rows = pl.ds(pl.multiple_of(block * 256, 256), 256)
        lhs = dyr_ref[block, :, :, :, last].reshape(256, QW)
        dh_acc[rows, :] = dh_acc[rows, :] + dot(lhs, down[:, last], NT)

        def block_grads(i, carry):
            return row_grads(block * 8 + i, carry)

        lax.fori_loop(0, 8, block_grads, 0, unroll=2)
        part_block(0, block)
        for turn in range(4):
            second = lax.rem(pos[1] + turn, 4)
            index = block * 4 + second
            device = place.on_plane(2, block, second)

            def away():
                remote(send.at[0, index], back.at[0, me_z], p_send.at[2, 0], p_recv.at[2, 0], device).start()

            if turn == 0:
                @pl.when(step == 0)
                def _():
                    pltpu.make_async_copy(send.at[0, index], back.at[0, me_z], p_local.at[2, 0]).start()

                pl.when(step > 0)(away)
            else:
                away()
        return carry

    lax.fori_loop(0, 4, first_back, 0)
    unfold(1, 3)
    dh_acc[1024:1152, :] = dh_acc[1024:1152, :] + dot(dy9_ref[:, last], down[:, last], NT)
    lax.fori_loop(32, 36, row_grads, 0)
    part_ninth(0)
    scatter(2, 0, main=False)
    def part_body(q):
        def body(block, carry):
            part_block(q, block)
            return carry

        return body

    for q in range(1, 4):
        sent(1, q)
        part_ninth(q)
        lax.fori_loop(0, 4, part_body(q), 0)
        scatter(2, q, main=q < 3)

    line_chips = [lax.rem(pos[AXES_PART[3]] + delta, 4) for delta in (2, 1, 3, 0)]
    me_last = place.plane(AXES_PART[3])
    for turn, chip in enumerate(line_chips):
        def chip_away(step, carry):
            device, index = plane_peer(place, AXES_PART[3], step)
            remote(
                send.at[3, index, chip], back.at[3, me_last, chip], c_send.at[turn], c_recv.at[turn], device
            ).start()
            return carry

        lax.fori_loop(1, 16, chip_away, 0)
        pltpu.make_async_copy(send.at[3, me_last, chip], back.at[3, me_last, chip], c_local.at[turn]).start()

    sums = jnp.sum(row_sum[0:1024, :].reshape(128, 8, 128), axis=1) + row_sum[1024:1152, :]
    gp_ref[...] = sums.reshape(16, 8, 128)

    def send_gp(step, carry):
        device, index = plane_peer(place, 2, step)
        remote(gp_ref.at[index], gp_recv.at[me_z], gp_sems.at[0], gp_sems.at[1], device).start()
        return carry

    lax.fori_loop(1, 16, send_gp, 0)
    pltpu.make_async_copy(gp_ref.at[me_z], gp_recv.at[me_z], gp_sems.at[1]).start()

    whole = gath.at[0, :, :, 0]
    pltpu.make_async_copy(whole, whole, g2_send.at[0]).wait()

    def weight_grads(quarter):
        for tile in (quarter * 2, quarter * 2 + 1):
            cols = slice(tile * 256, (tile + 1) * 256)
            lhs = xr_ref[:, :, :, :, cols].reshape(1024, 256)
            lhs9 = x9_ref[:, cols]
            for which, (rows_ref, buffer, out) in enumerate(((dg_ref, gate, ggate_hbm), (du_ref, up, gup_hbm))):
                value = dot(lhs, rows_ref[0:1024, :], TN) + dot(lhs9, rows_ref[1024:1152, :], TN)
                buffer[cols, :] = value.astype(BF)
                pltpu.make_async_copy(buffer.at[cols], out.at[cols], out_sem.at[which]).start()

    def own(q, chip):
        return pl.ds(pl.multiple_of(((q % 2) * 4 + chip) * 128, 128), 128)

    def combine_chip(q, chip, ready=None):
        build_select(rank_ref, None, AXES_PART[q], chip, main_sel, ninth_sel)
        if ready is not None:
            ready()
        last = back9[q].reshape(256, HW)
        value = dot(main_sel[...], back[q, :, chip].reshape(256, QW), TN)
        value = value + jnp.concatenate([dot(ninth_sel[0], last, TN), dot(ninth_sel[1], last, TN)], axis=1)
        mine = core == 0
        g_acc[own(q, chip), :QW] = jnp.where(mine, value[:128], value[128:])
        gath[0, q, chip, 0] = jnp.where(mine, value[128:], value[:128]).astype(BF)

    def combine(q):
        received(2, q)
        kept(2, q)
        for chip in range(4):
            combine_chip(q, chip)
        remote(gath.at[0, q, :, 0], mate_recv.at[q], m_send.at[q], m_recv.at[q], place.mate()).start()

    def to_line(q):
        axis = AXES_PART[q]
        whole = mate_recv.at[q]
        pltpu.make_async_copy(whole, whole, m_recv.at[q]).wait()
        for chip in range(4):
            gath[0, q, chip, 1] = (g_acc[own(q, chip), :QW] + mate_recv[q, chip].astype(F32)).astype(BF)
        for delta in (1, 3, 2):
            at = lax.rem(pos[axis] + delta, 4)
            remote(
                gath.at[0, q, at, 1], line_recv.at[q, pos[axis]], l_send.at[q], l_recv.at[q],
                place.on_axis(axis, at, core),
            ).start()
        pltpu.make_async_copy(gath.at[0, q, pos[axis], 1], line_recv.at[q, pos[axis]], l_recv.at[q]).start()

    def combine_last(turn):
        chip = line_chips[turn]

        def ready():
            whole = send.at[3, pl.ds(0, 15), 0]
            pltpu.make_async_copy(whole, whole, c_recv.at[turn]).wait()
            one = send.at[3, 0, 0]
            pltpu.make_async_copy(one, one, c_local.at[turn]).wait()

        combine_chip(3, chip, ready)
        remote(
            gath.at[0, 3, chip, 0], mate_recv.at[3, chip], mc_send.at[turn], mc_recv.at[turn], place.mate()
        ).start()

    def line_last(turn):
        chip = line_chips[turn]
        one = mate_recv.at[3, chip]
        pltpu.make_async_copy(one, one, mc_recv.at[turn]).wait()
        gath[0, 3, chip, 1] = (g_acc[own(3, chip), :QW] + mate_recv[3, chip].astype(F32)).astype(BF)
        here = line_recv.at[3, pos[AXES_PART[3]]]
        if turn < 3:
            device = place.on_axis(AXES_PART[3], chip, core)
            remote(gath.at[0, 3, chip, 1], here, l_send.at[3], l_recv.at[3], device).start()
        else:
            pltpu.make_async_copy(gath.at[0, 3, chip, 1], here, l_recv.at[3]).start()

    def finish(q):
        whole = line_recv.at[q]
        pltpu.make_async_copy(whole, whole, l_recv.at[q]).wait()
        total = line_recv[q, 0].astype(F32) + line_recv[q, 1].astype(F32)
        total = total + line_recv[q, 2].astype(F32) + line_recv[q, 3].astype(F32)
        gx_ref[:, q * QW:(q + 1) * QW] = total.astype(BF)

    def probs_back():
        pltpu.make_async_copy(gp_recv, gp_recv, gp_sems.at[1]).wait()
        expert = ((index_y * 4 + index_x) * 8 + pos[2] * 2 + core).astype(F32)
        for source in range(8):
            rank = rank_ref[16 + source]
            values = gp_recv[:, source, :]
            info = infos_ref[16 + source]
            spread = jnp.zeros((16, 128), F32)
            for j in range(9):
                spread = jnp.where(rank == j, values[:, j:j + 1], spread)
            for k in range(TOP):
                hit = info[k:k + 1, :] == expert
                gp_part[source, k:k + 1, :] = jnp.sum(jnp.where(hit, spread, 0.0), axis=0, keepdims=True)
        mine = pos[2] * 2 + core
        for delta in range(4):
            at = lax.rem(pos[2] + delta, 4)
            for whose in ((core, place.mate_core) if delta else (place.mate_core,)):
                remote(
                    gp_part.at[at * 2 + whose], gp_back.at[mine], gb_sems.at[0], gb_sems.at[1],
                    place.on_axis(2, at, whose),
                ).start()
        pltpu.make_async_copy(gp_part.at[mine], gp_back.at[mine], gb_sems.at[1]).start()

    index_x, index_y = lax.shift_right_logical(index, 2), lax.bitwise_and(index, 3)
    weight_grads(0)
    probs_back()
    combine(0)
    weight_grads(1)
    to_line(0)
    combine(1)
    weight_grads(2)
    to_line(1)
    combine(2)
    finish(0)
    to_line(2)
    received9(2, 3)
    combine_last(0)
    combine_last(1)
    line_last(0)
    combine_last(2)
    line_last(1)
    combine_last(3)
    line_last(2)
    line_last(3)
    finish(1)
    down_grads(3)
    weight_grads(3)
    pltpu.make_async_copy(gp_back, gp_back, gb_sems.at[1]).wait()
    total = gp_back[0]
    for i in range(1, 8):
        total = total + gp_back[i]
    gpt_ref[...] = total
    finish(2)

    for which, (buffer, out) in enumerate(((gate, ggate_hbm), (up, gup_hbm), (down, gdown_hbm))):
        pltpu.make_async_copy(buffer, out, out_sem.at[which]).wait()
    whole = infos_ref.at[pl.ds(0, 21)]
    pltpu.make_async_copy(whole, whole, info_send).wait()
    for arr in range(2):
        whole = gath.at[arr, :, pl.ds(0, 3), 0]
        pltpu.make_async_copy(whole, whole, g1_send.at[arr]).wait()
    whole = gath.at[1, :, :, 0]
    pltpu.make_async_copy(whole, whole, g2_send.at[1]).wait()
    whole = gp_recv.at[pl.ds(0, 15)]
    pltpu.make_async_copy(whole, whole, gp_sems.at[0]).wait()
    whole = gp_back.at[pl.ds(0, 7)]
    pltpu.make_async_copy(whole, whole, gb_sems.at[0]).wait()
    for q in range(3):
        sent(2, q)
        whole = mate_recv.at[q]
        pltpu.make_async_copy(whole, whole, m_send.at[q]).wait()
    whole = send9.at[3, pl.ds(0, 15)]
    pltpu.make_async_copy(whole, whole, p9_send.at[2, 3]).wait()
    for turn in range(4):
        whole = send.at[3, pl.ds(0, 15), 0]
        pltpu.make_async_copy(whole, whole, c_send.at[turn]).wait()
        one = mate_recv.at[3, 0]
        pltpu.make_async_copy(one, one, mc_send.at[turn]).wait()
    for q in range(4):
        whole = line_recv.at[q, pl.ds(0, 3)]
        pltpu.make_async_copy(whole, whole, l_send.at[q]).wait()
    finish(3)


def hand_over(
    gx_ref, gpt_ref, probs_ref, gate_ref, up_ref, down_ref, gx_out, probs_out, gate_out, up_out, down_out,
    gx, gate, up, down, in_sems, out_sems,
):
    steps = []
    for src, via, dst in (
        (gate_ref, gate, gate_out), (up_ref, up, up_out), (down_ref, down, down_out), (gx_ref, gx, gx_out)
    ):
        rows = max(src.shape[0] // 4, 128)
        for start in range(0, src.shape[0], rows):
            part, n = pl.ds(start, rows), len(steps)
            steps.append((
                pltpu.make_async_copy(src.at[part], via.at[part], in_sems.at[n]),
                pltpu.make_async_copy(via.at[part], dst.at[part], out_sems.at[n]),
            ))
    for load, _ in steps:
        load.start()
    probs_out[...] = (gpt_ref[...] / probs_ref[...].astype(F32)).astype(BF)
    for load, store in steps:
        load.wait()
        store.start()
    for _, store in steps:
        store.wait()


VMEM = pl.BlockSpec(memory_space=pltpu.VMEM)
ANY = pl.BlockSpec(memory_space=pl.ANY)
DMA = pltpu.SemaphoreType.DMA


def sds(*shape, dtype=BF):
    return jax.ShapeDtypeStruct(shape, dtype)


def shards(tokens_x, grad_out, expert_ids, probs, w_gate, w_up, w_down):
    ids_t, probs_t = expert_ids.T, probs.T
    table = jnp.asarray(unfold_table(), BF)
    grad_x, gpt, grad_gate, grad_up, grad_down = pl.pallas_call(
        kernel,
        out_shape=(
            sds(TOK, DIM), sds(TOP, TOK, dtype=F32), sds(DIM, HID), sds(DIM, HID), sds(HID, DIM),
        ),
        in_specs=[ANY, ANY, VMEM, VMEM, VMEM, ANY, ANY, ANY],
        out_specs=(VMEM, VMEM, ANY, ANY, ANY),
        scratch_shapes=[
            pltpu.VMEM((4, 4, 4, 16, DIM), BF),
            pltpu.VMEM((128, DIM), BF),
            pltpu.VMEM((4, 4, 4, 16, DIM), BF),
            pltpu.VMEM((128, DIM), BF),
            pltpu.VMEM((1152, HID), BF),
            pltpu.VMEM((1152, HID), BF),
            pltpu.VMEM((1152, HID), BF),
            pltpu.VMEM((16, 128), F32),
            pltpu.VMEM((24, 16, 128), jnp.int32),
            pltpu.VMEM((24, 16, 128), F32),
            pltpu.VMEM((24, 16, 128), F32),
            pltpu.VMEM((2, 4, 4, 2, TOK, QW), BF),
            pltpu.VMEM((4, 16, 4, 16, QW), BF),
            pltpu.VMEM((4, 16, 16, HW), BF),
            pltpu.VMEM((2, 4, 16, 16, HW), BF),
            pltpu.VMEM((256, 256), BF),
            pltpu.VMEM((2, 256, 256), BF),
            pltpu.VMEM((DIM, HID), BF),
            pltpu.VMEM((DIM, HID), BF),
            pltpu.VMEM((HID, DIM), BF),
            pltpu.VMEM((1152, HID), F32),
            pltpu.VMEM((1152, HID), F32),
            pltpu.VMEM((1152, HID), F32),
            pltpu.VMEM((1152, 128), F32),
            pltpu.VMEM((4, 16, 4, 16, QW), BF),
            pltpu.VMEM((4, 16, 16, HW), BF),
            pltpu.VMEM((4, 4, TOK, QW), BF),
            pltpu.VMEM((4, 4, TOK, QW), BF),
            pltpu.VMEM((16, 8, 128), F32),
            pltpu.VMEM((16, 8, 128), F32),
            pltpu.VMEM((8, 8, 128), F32),
            pltpu.VMEM((8, 8, 128), F32),
            DMA((3,)), DMA, DMA, DMA((2,)), DMA((2, 4, 4)), DMA((2,)), DMA((2, 4, 4)),
            DMA((3, 4)), DMA((3, 4)), DMA((3, 4)), DMA((3, 4)),
            DMA((3, 4)), DMA((3, 4)), DMA((4,)), DMA((4,)), DMA((4,)), DMA((4,)), DMA((4,)),
            DMA((4,)), DMA((4,)), DMA((4,)), DMA((4,)), DMA((2,)), DMA((2,)), DMA((3,)),
        ],
        compiler_params=pltpu.CompilerParams(
            collective_id=1, has_side_effects=True, vmem_limit_bytes=62 << 20
        ),
        cost_estimate=pl.CostEstimate(flops=30 << 30, bytes_accessed=30 << 20, transcendentals=1 << 20),
    )(tokens_x, grad_out, ids_t, probs_t, table, w_gate[0], w_up[0], w_down[0])
    grad_x, gpt, grad_gate, grad_up, grad_down = pl.pallas_call(
        hand_over,
        out_shape=(sds(TOK, DIM), sds(TOP, TOK), sds(DIM, HID), sds(DIM, HID), sds(HID, DIM)),
        in_specs=[ANY, VMEM, VMEM, ANY, ANY, ANY],
        out_specs=(ANY, VMEM, ANY, ANY, ANY),
        scratch_shapes=[
            pltpu.VMEM((TOK, DIM), BF),
            pltpu.VMEM((DIM, HID), BF),
            pltpu.VMEM((DIM, HID), BF),
            pltpu.VMEM((HID, DIM), BF),
            DMA((13,)), DMA((13,)),
        ],
        compiler_params=pltpu.CompilerParams(vmem_limit_bytes=60 << 20),
        cost_estimate=pl.CostEstimate(flops=1024, bytes_accessed=20 << 20, transcendentals=0),
    )(grad_x, gpt, probs_t, grad_gate, grad_up, grad_down)
    return grad_x, gpt.T, grad_gate[None], grad_up[None], grad_down[None]


def solution(mesh):
    token = P(("node", "local"), None)
    weight = P(("node", "local"), None, None)
    return jax.shard_map(
        shards,
        mesh=mesh,
        in_specs=(token, token, token, token, weight, weight, weight),
        out_specs=(token, token, weight, weight, weight),
        check_vma=False,
    )
```
